256 devices in a mesh: lat: 8 (over y_lo, x), lon: 32 (over y_hi, z, core).
Axes of the slice: x: 4, y: 4 (y_hi: 2, y_lo: 2; y = y_hi * 2 + y_lo), z: 8, core: 2. Of those that a mesh axis runs over, the one named last changes fastest.
Arguments:
- latent_field: bfloat16 [48, 384, 4, 512], P('lat', 'lon'), may hold values from -6 to 6
- gain_win: float32 [512], replicated, may hold values from 0.1 to 1.9
- w_qkv_win: bfloat16 [512, 1536], replicated, may hold values from -24 to 24
- w_out_win: bfloat16 [512, 512], replicated, may hold values from -0.25 to 0.25
- gain_shift: float32 [512], replicated, may hold values from 0.1 to 1.9
- w_qkv_shift: bfloat16 [512, 1536], replicated, may hold values from -24 to 24
- w_out_shift: bfloat16 [512, 512], replicated, may hold values from -0.25 to 0.25
- gain_mlp: float32 [512], replicated, may hold values from 0.1 to 1.9
- w_up: bfloat16 [512, 2048], replicated, may hold values from -0.25 to 0.25
- w_down: bfloat16 [2048, 512], replicated, may hold values from -0.125 to 0.125
- gain_merge: float32 [2048], replicated, may hold values from 0.1 to 1.9
- w_merge: bfloat16 [2048, 1024], replicated, may hold values from -0.125 to 0.125
Outputs:
- merged: bfloat16 [24, 192, 4, 1024], P('lat', 'lon')
The draws below stay inside these ranges and needn't reach their ends.
All inputs are finite; a program needn't handle non-finite values.
Results may differ from the reference program's by a relative error of at most 0.017.
Values may be sent and summed in bfloat16 or wider, within the bound.
No kernel may reach another device: no remote copies, remote signals or barrier semaphores. Data moves between devices by JAX's collectives and lax.ppermute only.
A program may use at most 128 MiB of HBM per device.

```python
import math
import jax
import jax.numpy as jnp
from jax import lax

D = 512
HEADS = 16
HEAD = 32
FF = 2048
LEV = 4
WLAT = 6
WLON = 12
WLEV = 2
NLAT = 48
NLON = 384


def attention_weights(key, share, strength_lo, strength_hi):
    base_key, pick_key, strength_key = jax.random.split(key, 3)
    base_draw = jax.random.normal(base_key, (D, 3 * D), jnp.float32) / math.sqrt(D)
    query_cols = base_draw[:, :D]
    chosen = jax.random.bernoulli(pick_key, share, (HEADS,))
    strength = jax.random.uniform(strength_key, (HEADS,), jnp.float32, strength_lo, strength_hi)
    column_strength = jnp.repeat(strength, HEAD)
    column_pick = jnp.repeat(chosen, HEAD)
    key_cols = jnp.where(column_pick[None, :], query_cols * column_strength[None, :], base_draw[:, D:2 * D])
    return jnp.concatenate([query_cols, key_cols, base_draw[:, 2 * D:]], axis=1).astype(jnp.bfloat16)


def draw_w_qkv_win(key, part):
    key = jax.random.fold_in(key, 11)
    return attention_weights(key, 0.0, 1.0, 1.0)


def draw_w_qkv_shift(key, part):
    key = jax.random.fold_in(key, 23)
    return attention_weights(key, 0.0, 1.0, 1.0)


def steps_of(own_key, extent, shards, low, top_value):
    def one(axis_at, blocks):
        steps = jax.random.uniform(jax.random.fold_in(jax.random.fold_in(own_key, 6), axis_at), (blocks,), jnp.float32, low / len(shards), top_value / len(shards))
        return jnp.repeat(jnp.exp(steps), extent[axis_at] // blocks).reshape((-1,) + (1,) * (len(extent) - axis_at - 1))

    level = one(*shards[0])
    for cut in shards[1:]:
        level = level * one(*cut)
    return level


def centred(rng, extent, deviation, limit, pieces=(), held_as=jnp.bfloat16):
    level = steps_of(rng, extent, pieces, -0.22, 0.18) if pieces else 1.0
    entries = jax.random.normal(rng, extent, jnp.float32) * deviation * level
    return jnp.minimum(jnp.maximum(entries, -limit), limit).astype(held_as)


def setup_inputs(seed: int = 0) -> dict:
    keys = jax.random.split(jax.random.key(seed), 13)
    return {
        "latent_field": centred(keys[0], (NLAT, NLON, LEV, D), 1.0, 6.0, ((0, 8), (1, 32))),
        "gain_win": jnp.clip(1.0 + 0.18 * jax.random.normal(keys[1], (D,), jnp.float32), 0.1, 1.9),
        "w_qkv_win": draw_w_qkv_win(jax.random.fold_in(keys[12], 71), 0),
        "w_out_win": centred(keys[3], (D, D), D ** -0.5, 0.25),
        "gain_shift": jnp.clip(1.0 + 0.18 * jax.random.normal(keys[4], (D,), jnp.float32), 0.1, 1.9),
        "w_qkv_shift": draw_w_qkv_shift(jax.random.fold_in(keys[12], 71), 0),
        "w_out_shift": centred(keys[6], (D, D), D ** -0.5, 0.25),
        "gain_mlp": jnp.clip(1.0 + 0.18 * jax.random.normal(keys[7], (D,), jnp.float32), 0.1, 1.9),
        "w_up": centred(keys[8], (D, FF), D ** -0.5, 0.25),
        "w_down": centred(keys[9], (FF, D), FF ** -0.5, 0.125),
        "gain_merge": jnp.clip(1.0 + 0.18 * jax.random.normal(keys[10], (4 * D,), jnp.float32), 0.1, 1.9),
        "w_merge": centred(keys[11], (4 * D, 2 * D), (4 * D) ** -0.5, 0.125),
    }


epsilon = 1e-05

def layer_norm(values, gain_vec):
    values = values.astype(jnp.float32)
    centered = values - lax.optimization_barrier(jnp.mean(values, axis=-1, keepdims=True))
    spread = lax.optimization_barrier(jnp.mean(centered * centered, axis=-1, keepdims=True))
    return centered * lax.rsqrt(spread + epsilon) * gain_vec

def to_windows(grid_values):
    row_count, col_count, level_count, channels = grid_values.shape
    blocked = grid_values.reshape(row_count // WLAT, WLAT, col_count // WLON, WLON, level_count // WLEV, WLEV, channels)
    blocked = blocked.transpose(0, 2, 4, 1, 3, 5, 6)
    return blocked.reshape(-1, WLAT * WLON * WLEV, channels)

def from_windows(windows, row_count, col_count, level_count):
    channels = windows.shape[-1]
    blocked = windows.reshape(row_count // WLAT, col_count // WLON, level_count // WLEV, WLAT, WLON, WLEV, channels)
    blocked = blocked.transpose(0, 3, 1, 4, 2, 5, 6)
    return blocked.reshape(row_count, col_count, level_count, channels)

def window_attention(normed, labels, w_qkv, w_out):
    row_count, col_count, level_count, width = normed.shape
    windows = to_windows(normed)
    win_count, win_size = (windows.shape[0], windows.shape[1])
    projected = jnp.dot(windows.reshape(win_count * win_size, width), w_qkv, preferred_element_type=jnp.float32).astype(jnp.bfloat16)
    projected = projected.reshape(win_count, win_size, 3, HEADS, HEAD).astype(jnp.float32)
    scores = jnp.einsum('wshd,wthd->whst', projected[:, :, 0], projected[:, :, 1]) * (1.0 / math.sqrt(HEAD))
    window_labels = to_windows(labels[..., None])[..., 0]
    allowed = (window_labels[:, :, None] == window_labels[:, None, :])[:, None]
    scores = jnp.where(allowed, scores, jnp.float32(-1e+30))
    row_max = lax.optimization_barrier(jnp.max(scores, axis=-1, keepdims=True))
    weights = jnp.exp(scores - row_max)
    probabilities = (weights / lax.optimization_barrier(jnp.sum(weights, axis=-1, keepdims=True))).astype(jnp.bfloat16)
    context = jnp.einsum('whst,wthd->wshd', probabilities.astype(jnp.float32), projected[:, :, 2]).astype(jnp.bfloat16)
    projection = jnp.dot(context.reshape(win_count * win_size, width), w_out, preferred_element_type=jnp.float32)
    return from_windows(projection.reshape(win_count, win_size, width), row_count, col_count, level_count)

def band_attention(normed, labels, w_qkv, w_out):
    total_lat, total_lon, level_count, width = normed.shape
    band_grid = normed.reshape(total_lat // WLAT, WLAT, total_lon, level_count, width)
    band_labels = labels.reshape(total_lat // WLAT, WLAT, total_lon, level_count)

    def attend_band(band_pair):
        return window_attention(band_pair[0], band_pair[1], w_qkv, w_out)
    result = lax.map(attend_band, (band_grid, band_labels))
    return result.reshape(total_lat, total_lon, level_count, width)

def merge_patches(grid_values, gain_vec, weight):
    row_count, col_count, level_count, channels = grid_values.shape
    blocked = grid_values.reshape(row_count // 2, 2, col_count // 2, 2, level_count, channels)
    stacked = blocked.transpose(0, 2, 4, 3, 1, 5).reshape(row_count // 2, col_count // 2, level_count, 4 * channels)
    normed = layer_norm(stacked, gain_vec).astype(jnp.bfloat16)
    result = jnp.dot(normed.reshape(-1, 4 * channels), weight, preferred_element_type=jnp.float32)
    return result.reshape(row_count // 2, col_count // 2, level_count, 2 * channels).astype(jnp.bfloat16)

def reference(latent_field, gain_win, w_qkv_win, w_out_win, gain_shift, w_qkv_shift, w_out_shift, gain_mlp, w_up, w_down, gain_merge, w_merge):
    total_lat, total_lon, level_count, width = latent_field.shape
    half_lat, half_lon, half_lev = (WLAT // 2, WLON // 2, WLEV // 2)
    zero_labels = jnp.zeros((total_lat, total_lon, level_count), jnp.int32)
    normed = layer_norm(latent_field, gain_win).astype(jnp.bfloat16)
    after_window = (latent_field.astype(jnp.float32) + band_attention(normed, zero_labels, w_qkv_win, w_out_win)).astype(jnp.bfloat16)
    rolled = jnp.roll(after_window, (-half_lat, -half_lon, -half_lev), axis=(0, 1, 2))
    lat_label = (jnp.arange(total_lat) >= total_lat - half_lat).astype(jnp.int32)
    lev_label = (jnp.arange(level_count) >= level_count - half_lev).astype(jnp.int32)
    labels = 2 * lat_label[:, None, None] + lev_label[None, None, :] + jnp.zeros((total_lat, total_lon, level_count), jnp.int32)
    normed = layer_norm(rolled, gain_shift).astype(jnp.bfloat16)
    branch = band_attention(normed, labels, w_qkv_shift, w_out_shift).astype(jnp.bfloat16)
    branch = lax.optimization_barrier(branch)
    branch = jnp.roll(branch, (half_lat, half_lon, half_lev), axis=(0, 1, 2))
    after_shift = (after_window.astype(jnp.float32) + branch.astype(jnp.float32)).astype(jnp.bfloat16)
    normed = layer_norm(after_shift, gain_mlp).astype(jnp.bfloat16).reshape(-1, width)
    hidden = jax.nn.gelu(jnp.dot(normed, w_up, preferred_element_type=jnp.float32)).astype(jnp.bfloat16)
    down = jnp.dot(hidden, w_down, preferred_element_type=jnp.float32).reshape(after_shift.shape)
    after_mlp = (after_shift.astype(jnp.float32) + down).astype(jnp.bfloat16)
    return merge_patches(after_mlp, gain_merge, w_merge)
```

```python
import functools
import math

import jax
import jax.numpy as jnp
import numpy as np
from jax import lax
from jax.experimental import pallas as pl
from jax.experimental.pallas import tpu as pltpu
from jax.sharding import PartitionSpec as P

HEADS = 16
HEAD = 32
WLAT = 6
WLON = 12
WLEV = 2
LEV = 4
HALF_LAT = WLAT // 2
HALF_LON = WLON // 2
WIN = WLAT * WLON * WLEV
TOKENS = WLAT * WLON * LEV
QUAD = TOKENS // 4
GROUP = 8
LANES = GROUP * HEAD

epsilon = 1e-05


def _quadrant_tokens():
    return [
        (half_r * HALF_LAT + r, half_c * HALF_LON + c, l)
        for half_r in range(2)
        for half_c in range(2)
        for l in range(LEV)
        for r in range(HALF_LAT)
        for c in range(HALF_LON)
    ]


def _window_tokens(level_order):
    return [
        (r, c, l) for l in level_order for r in range(WLAT) for c in range(WLON)
    ]


def _permutation(target, source):
    place = {token: index for index, token in enumerate(source)}
    matrix = np.zeros((len(target), len(source)), np.float32)
    for index, token in enumerate(target):
        matrix[index, place[token]] = 1.0
    return jnp.asarray(matrix, jnp.bfloat16)


def _natural_tokens():
    return [(r, c, l) for r in range(WLAT) for c in range(WLON) for l in range(LEV)]


def _merge_tokens():
    return [
        (2 * i + piece % 2, 2 * j + piece // 2, l)
        for piece in range(4)
        for i in range(WLAT // 2)
        for j in range(WLON // 2)
        for l in range(LEV)
    ]


def normed(values, gain_row):
    centered = values - jnp.mean(values, axis=-1, keepdims=True)
    spread = jnp.mean(centered * centered, axis=-1, keepdims=True)
    return centered * lax.rsqrt(spread + epsilon) * gain_row


def permuted(matrix, values):
    return jnp.dot(matrix, values, preferred_element_type=jnp.float32).astype(jnp.bfloat16)


def attention(tokens, w_qkv, w_out, allowed):
    width = tokens.shape[-1]
    scale = math.log2(math.e) / math.sqrt(HEAD)
    query = jnp.dot(tokens, w_qkv[:, :width], preferred_element_type=jnp.float32).astype(
        jnp.bfloat16
    )
    key = jnp.dot(
        tokens, w_qkv[:, width : 2 * width], preferred_element_type=jnp.float32
    ).astype(jnp.bfloat16)
    value = jnp.dot(
        tokens, w_qkv[:, 2 * width :], preferred_element_type=jnp.float32
    ).astype(jnp.bfloat16)
    lane = lax.broadcasted_iota(jnp.int32, (WIN, LANES), 1)
    masks = [
        ((lane >= h * HEAD) & (lane < (h + 1) * HEAD)).astype(jnp.float32).astype(jnp.bfloat16)
        for h in range(GROUP)
    ]
    contexts = []
    for w in range(TOKENS // WIN):
        parts = []
        for g in range(HEADS // GROUP):
            rows = slice(w * WIN, (w + 1) * WIN)
            cols = slice(g * LANES, (g + 1) * LANES)
            q, k, v = query[rows, cols], key[rows, cols], value[rows, cols]
            stacked = jnp.concatenate([q * m for m in masks], axis=0)
            scores = lax.dot_general(
                k, stacked, (((1,), (1,)), ((), ())), preferred_element_type=jnp.float32
            )
            if allowed is not None:
                scores = jnp.where(allowed(w), scores, jnp.float32(-1e30))
            weights = jnp.exp2((scores - jnp.max(scores, axis=0, keepdims=True)) * scale)
            probs = (weights * (1.0 / jnp.sum(weights, axis=0, keepdims=True))).astype(
                jnp.bfloat16
            )
            mixed = lax.dot_general(
                probs, v, (((0,), (0,)), ((), ())), preferred_element_type=jnp.float32
            )
            context = mixed[:WIN]
            for h in range(1, GROUP):
                context = jnp.where(lane >= h * HEAD, mixed[h * WIN : (h + 1) * WIN], context)
            parts.append(context.astype(jnp.bfloat16))
        contexts.append(jnp.concatenate(parts, axis=1))
    context = jnp.concatenate(contexts, axis=0)
    return jnp.dot(context, w_out, preferred_element_type=jnp.float32)


def window_kernel(x_ref, to_win_ref, to_quad_ref, gain_ref, w_qkv_ref, w_out_ref, *outs):
    x = x_ref[...].astype(jnp.float32).reshape(TOKENS, x_ref.shape[-1]).astype(jnp.bfloat16)
    x = jnp.dot(to_win_ref[...], x, preferred_element_type=jnp.float32)
    tokens = normed(x, gain_ref[...]).astype(jnp.bfloat16)
    after = (x + attention(tokens, w_qkv_ref[...], w_out_ref[...], None)).astype(jnp.bfloat16)
    after = jnp.dot(to_quad_ref[...], after, preferred_element_type=jnp.float32)
    for index, out in enumerate(outs):
        out[...] = after[index * QUAD : (index + 1) * QUAD].astype(jnp.bfloat16)


def shift_kernel(
    last_ref, a_ref, b_ref, c_ref, d_ref, to_win_ref, to_quad_ref, gain_ref, w_qkv_ref, w_out_ref, *outs
):
    x = jnp.concatenate(
        [ref[...].astype(jnp.float32) for ref in (a_ref, b_ref, c_ref, d_ref)], axis=0
    )
    tokens = normed(x, gain_ref[...]).astype(jnp.bfloat16)
    tokens = permuted(to_win_ref[...], tokens)
    last = last_ref[0, 0]
    half = WIN // WLEV

    def code(position, w):
        level = (position >= half).astype(jnp.int32) if w == 1 else 0
        southern = (lax.rem(position, half) >= half // 2).astype(jnp.int32)
        return level + 2 * last * southern

    def allowed(w):
        shape = (WIN, GROUP * WIN)
        of_key = code(lax.broadcasted_iota(jnp.int32, shape, 0), w)
        of_query = code(lax.rem(lax.broadcasted_iota(jnp.int32, shape, 1), WIN), w)
        return of_key == of_query

    branch = attention(tokens, w_qkv_ref[...], w_out_ref[...], allowed).astype(jnp.bfloat16)
    branch = jnp.dot(to_quad_ref[...], branch, preferred_element_type=jnp.float32)
    for index, out in enumerate(outs):
        out[...] = branch[index * QUAD : (index + 1) * QUAD].astype(jnp.bfloat16)


def merge_kernel(
    a0, a1, a2, a3, b0, b1, b2, b3, to_merge_ref, gain_mlp_ref, w_up_ref, w_down_ref, gain_merge_ref, w_merge_ref, out_ref
):
    after = jnp.concatenate([ref[...].astype(jnp.float32) for ref in (a0, a1, a2, a3)], axis=0)
    branch = jnp.concatenate([ref[...].astype(jnp.float32) for ref in (b0, b1, b2, b3)], axis=0)
    shift = (after + branch).astype(jnp.bfloat16).astype(jnp.float32)
    tokens = normed(shift, gain_mlp_ref[...]).astype(jnp.bfloat16)
    hidden = jax.nn.gelu(
        jnp.dot(tokens, w_up_ref[...], preferred_element_type=jnp.float32), approximate=True
    ).astype(jnp.bfloat16)
    after_mlp = (
        shift + jnp.dot(hidden, w_down_ref[...], preferred_element_type=jnp.float32)
    ).astype(jnp.bfloat16)
    pieces = jnp.dot(to_merge_ref[...], after_mlp, preferred_element_type=jnp.float32)
    stacked = jnp.concatenate(
        [pieces[index * QUAD : (index + 1) * QUAD] for index in range(4)], axis=1
    )
    tokens = normed(stacked, gain_merge_ref[...]).astype(jnp.bfloat16)
    merged = jnp.dot(tokens, w_merge_ref[...], preferred_element_type=jnp.float32)
    out_ref[...] = merged.reshape(out_ref.shape).astype(jnp.bfloat16)


def _call(kernel, operands, out_shape, smem=()):
    return pl.pallas_call(
        kernel,
        out_shape=out_shape,
        in_specs=[
            pl.BlockSpec(memory_space=pltpu.SMEM if index in smem else pltpu.VMEM)
            for index in range(len(operands))
        ],
        out_specs=jax.tree.map(lambda _: pl.BlockSpec(memory_space=pltpu.VMEM), out_shape),
        compiler_params=pltpu.CompilerParams(vmem_limit_bytes=56 * 1024 * 1024),
    )(*operands)


def _fetched(value, rows, cols):
    lats, lons = lax.axis_size("lat"), lax.axis_size("lon")
    if not rows:
        return lax.ppermute(value, "lon", [((j + cols) % lons, j) for j in range(lons)])
    if not cols:
        return lax.ppermute(value, "lat", [((i + rows) % lats, i) for i in range(lats)])
    pairs = [
        (((i + rows) % lats) * lons + (j + cols) % lons, i * lons + j)
        for i in range(lats)
        for j in range(lons)
    ]
    return lax.ppermute(value, ("lat", "lon"), pairs)


def on_device(
    latent_field, gain_win, w_qkv_win, w_out_win, gain_shift, w_qkv_shift, w_out_shift,
    gain_mlp, w_up, w_down, gain_merge, w_merge,
):
    width = latent_field.shape[-1]
    quad = jax.ShapeDtypeStruct((QUAD, width), jnp.bfloat16)
    quads = _quadrant_tokens()
    plain = _window_tokens((0, 1, 2, 3))
    rolled = _window_tokens((1, 2, 3, 0))
    last = (lax.axis_index("lat") == lax.axis_size("lat") - 1).astype(jnp.int32).reshape(1, 1)

    x = latent_field.reshape(WLAT * WLON, LEV, width)
    nw, ne, sw, se = _call(
        window_kernel,
        (
            x, _permutation(plain, _natural_tokens()), _permutation(quads, plain),
            gain_win.reshape(1, -1), w_qkv_win, w_out_win,
        ),
        (quad,) * 4,
    )
    east = _fetched(sw, 0, 1)
    south = _fetched(ne, 1, 0)
    corner = _fetched(nw, 1, 1)
    own, to_east, to_south, to_corner = _call(
        shift_kernel,
        (
            last, se, east, south, corner, _permutation(rolled, quads),
            _permutation(quads, rolled), gain_shift.reshape(1, -1), w_qkv_shift, w_out_shift,
        ),
        (quad,) * 4,
        smem=(0,),
    )
    b_sw = _fetched(to_east, 0, -1)
    b_ne = _fetched(to_south, -1, 0)
    b_nw = _fetched(to_corner, -1, -1)
    merged = _call(
        merge_kernel,
        (
            nw, ne, sw, se, b_nw, b_ne, b_sw, own, _permutation(_merge_tokens(), quads),
            gain_mlp.reshape(1, -1), w_up, w_down, gain_merge.reshape(1, -1), w_merge,
        ),
        jax.ShapeDtypeStruct((QUAD // LEV, LEV, 2 * width), jnp.bfloat16),
    )
    return merged.reshape(WLAT // 2, WLON // 2, LEV, 2 * width)


def solution(mesh):
    in_specs = (P("lat", "lon", None, None),) + (P(),) * 11
    return jax.shard_map(
        on_device,
        mesh=mesh,
        in_specs=in_specs,
        out_specs=P("lat", "lon", None, None),
        check_vma=False,
    )
```

```python
import functools
import math

import jax
import jax.numpy as jnp
import numpy as np
from jax import lax
from jax.experimental import pallas as pl
from jax.experimental.pallas import tpu as pltpu
from jax.sharding import PartitionSpec as P

HEADS = 16
HEAD = 32
WLAT = 6
WLON = 12
WLEV = 2
LEV = 4
HALF_LAT = WLAT // 2
HALF_LON = WLON // 2
WIN = WLAT * WLON * WLEV
TOKENS = WLAT * WLON * LEV
QUAD = TOKENS // 4
GROUP = 8
LANES = GROUP * HEAD
VMEM_BYTES = 16 * 1024 * 1024

epsilon = 1e-05


def _quadrant_tokens():
    return [
        (half_r * HALF_LAT + r, half_c * HALF_LON + c, l)
        for half_r in range(2)
        for half_c in range(2)
        for l in range(LEV)
        for r in range(HALF_LAT)
        for c in range(HALF_LON)
    ]


def _window_tokens(level_order):
    return [
        (r, c, l) for l in level_order for r in range(WLAT) for c in range(WLON)
    ]


def _permutation(target, source):
    place = {token: index for index, token in enumerate(source)}
    matrix = np.zeros((len(target), len(source)), np.float32)
    for index, token in enumerate(target):
        matrix[index, place[token]] = 1.0
    return jnp.asarray(matrix, jnp.bfloat16)


def _natural_tokens():
    return [(r, c, l) for r in range(WLAT) for c in range(WLON) for l in range(LEV)]


def _merge_tokens():
    return [
        (2 * i + piece % 2, 2 * j + piece // 2, l)
        for piece in range(4)
        for i in range(WLAT // 2)
        for j in range(WLON // 2)
        for l in range(LEV)
    ]


def normed(values, gain_row):
    centered = values - jnp.mean(values, axis=-1, keepdims=True)
    spread = jnp.mean(centered * centered, axis=-1, keepdims=True)
    return centered * lax.rsqrt(spread + epsilon) * gain_row


def permuted(matrix, values):
    return jnp.dot(matrix, values, preferred_element_type=jnp.float32).astype(jnp.bfloat16)


def attention(tokens, w_qkv, w_out, allowed):
    width = tokens.shape[-1]
    scale = math.log2(math.e) / math.sqrt(HEAD)
    query = jnp.dot(tokens, w_qkv[:, :width], preferred_element_type=jnp.float32).astype(
        jnp.bfloat16
    )
    key = jnp.dot(
        tokens, w_qkv[:, width : 2 * width], preferred_element_type=jnp.float32
    ).astype(jnp.bfloat16)
    value = jnp.dot(
        tokens, w_qkv[:, 2 * width :], preferred_element_type=jnp.float32
    ).astype(jnp.bfloat16)
    lane = lax.broadcasted_iota(jnp.int32, (WIN, LANES), 1)
    masks = [
        ((lane >= h * HEAD) & (lane < (h + 1) * HEAD)).astype(jnp.float32).astype(jnp.bfloat16)
        for h in range(GROUP)
    ]
    contexts = []
    for w in range(TOKENS // WIN):
        parts = []
        for g in range(HEADS // GROUP):
            rows = slice(w * WIN, (w + 1) * WIN)
            cols = slice(g * LANES, (g + 1) * LANES)
            q, k, v = query[rows, cols], key[rows, cols], value[rows, cols]
            stacked = jnp.concatenate([q * m for m in masks], axis=0)
            scores = lax.dot_general(
                k, stacked, (((1,), (1,)), ((), ())), preferred_element_type=jnp.float32
            )
            if allowed is not None:
                scores = jnp.where(allowed(w), scores, jnp.float32(-1e30))
            weights = jnp.exp2((scores - jnp.max(scores, axis=0, keepdims=True)) * scale)
            probs = (weights * (1.0 / jnp.sum(weights, axis=0, keepdims=True))).astype(
                jnp.bfloat16
            )
            mixed = lax.dot_general(
                probs, v, (((0,), (0,)), ((), ())), preferred_element_type=jnp.float32
            )
            context = mixed[:WIN]
            for h in range(1, GROUP):
                context = jnp.where(lane >= h * HEAD, mixed[h * WIN : (h + 1) * WIN], context)
            parts.append(context.astype(jnp.bfloat16))
        contexts.append(jnp.concatenate(parts, axis=1))
    context = jnp.concatenate(contexts, axis=0)
    return jnp.dot(context, w_out, preferred_element_type=jnp.float32)


def window_kernel(
    x_hbm, to_win_hbm, to_quad_hbm, gain_hbm, w_qkv_hbm, w_out_hbm, *refs
):
    outs, held, sems = refs[:4], refs[4:-1], refs[-1]
    sources = (x_hbm, to_win_hbm, gain_hbm, w_qkv_hbm, w_out_hbm, to_quad_hbm)
    copies = [
        pltpu.make_async_copy(source, target, sems.at[index])
        for index, (source, target) in enumerate(zip(sources, held))
    ]
    for copy in copies:
        copy.start()
    x_ref, to_win_ref, gain_ref, w_qkv_ref, w_out_ref, to_quad_ref = held
    for copy in copies:
        copy.wait()
    x = x_ref[...].astype(jnp.float32).reshape(TOKENS, x_ref.shape[-1]).astype(jnp.bfloat16)
    x = jnp.dot(to_win_ref[...], x, preferred_element_type=jnp.float32)
    tokens = normed(x, gain_ref[...]).astype(jnp.bfloat16)
    after = (x + attention(tokens, w_qkv_ref[...], w_out_ref[...], None)).astype(jnp.bfloat16)
    after = jnp.dot(to_quad_ref[...], after, preferred_element_type=jnp.float32)
    for index, out in enumerate(outs):
        out[...] = after[index * QUAD : (index + 1) * QUAD].astype(jnp.bfloat16)


def shift_kernel(
    last_ref, a_ref, b_ref, c_ref, d_ref, to_win_ref, to_quad_ref, gain_ref, w_qkv_ref, w_out_ref, *outs
):
    x = jnp.concatenate(
        [ref[...].astype(jnp.float32) for ref in (a_ref, b_ref, c_ref, d_ref)], axis=0
    )
    tokens = normed(x, gain_ref[...]).astype(jnp.bfloat16)
    tokens = permuted(to_win_ref[...], tokens)
    last = last_ref[0, 0]
    half = WIN // WLEV

    def code(position, w):
        level = (position >= half).astype(jnp.int32) if w == 1 else 0
        southern = (lax.rem(position, half) >= half // 2).astype(jnp.int32)
        return level + 2 * last * southern

    def allowed(w):
        shape = (WIN, GROUP * WIN)
        of_key = code(lax.broadcasted_iota(jnp.int32, shape, 0), w)
        of_query = code(lax.rem(lax.broadcasted_iota(jnp.int32, shape, 1), WIN), w)
        return of_key == of_query

    branch = attention(tokens, w_qkv_ref[...], w_out_ref[...], allowed).astype(jnp.bfloat16)
    branch = jnp.dot(to_quad_ref[...], branch, preferred_element_type=jnp.float32)
    for index, out in enumerate(outs):
        out[...] = branch[index * QUAD : (index + 1) * QUAD].astype(jnp.bfloat16)


def merge_kernel(
    a0, a1, a2, a3, b0, b1, b2, b3, to_merge_ref, gain_mlp_ref, w_up_ref, w_down_ref, gain_merge_ref, w_merge_ref, out_ref
):
    after = jnp.concatenate([ref[...].astype(jnp.float32) for ref in (a0, a1, a2, a3)], axis=0)
    branch = jnp.concatenate([ref[...].astype(jnp.float32) for ref in (b0, b1, b2, b3)], axis=0)
    shift = (after + branch).astype(jnp.bfloat16).astype(jnp.float32)
    tokens = normed(shift, gain_mlp_ref[...]).astype(jnp.bfloat16)
    hidden = jax.nn.gelu(
        jnp.dot(tokens, w_up_ref[...], preferred_element_type=jnp.float32), approximate=True
    ).astype(jnp.bfloat16)
    after_mlp = (
        shift + jnp.dot(hidden, w_down_ref[...], preferred_element_type=jnp.float32)
    ).astype(jnp.bfloat16)
    pieces = jnp.dot(to_merge_ref[...], after_mlp, preferred_element_type=jnp.float32)
    stacked = jnp.concatenate(
        [pieces[index * QUAD : (index + 1) * QUAD] for index in range(4)], axis=1
    )
    tokens = normed(stacked, gain_merge_ref[...]).astype(jnp.bfloat16)
    merged = jnp.dot(tokens, w_merge_ref[...], preferred_element_type=jnp.float32)
    out_ref[...] = merged.reshape(out_ref.shape).astype(jnp.bfloat16)


def _in_hbm(array):
    return pltpu.with_memory_space_constraint(array, pltpu.HBM)


def prefetch_kernel(*refs):
    count = (len(refs) - 2) // 2
    sources, targets, sems = refs[1 : 1 + count], refs[1 + count : -1], refs[-1]
    copies = [
        pltpu.make_async_copy(source, target, sems.at[index])
        for index, (source, target) in enumerate(zip(sources, targets))
    ]
    for copy in copies:
        copy.start()
    for copy in copies:
        copy.wait()


def _prefetched(after, arrays):
    return pl.pallas_call(
        prefetch_kernel,
        out_shape=[pltpu.VMEM(array.shape, array.dtype) for array in arrays],
        in_specs=[pl.BlockSpec(memory_space=pl.ANY)] + [pl.BlockSpec(memory_space=pltpu.HBM)] * len(arrays),
        out_specs=[pl.BlockSpec(memory_space=pltpu.VMEM)] * len(arrays),
        scratch_shapes=[pltpu.SemaphoreType.DMA((len(arrays),))],
        compiler_params=pltpu.CompilerParams(vmem_limit_bytes=VMEM_BYTES),
        cost_estimate=pl.CostEstimate(flops=0, bytes_accessed=24 * 1024 * 1024, transcendentals=0),
    )(after, *map(_in_hbm, arrays))


def _call(kernel, operands, out_shape, smem=()):
    return pl.pallas_call(
        kernel,
        out_shape=out_shape,
        in_specs=[
            pl.BlockSpec(memory_space=pltpu.SMEM if index in smem else pltpu.VMEM)
            for index in range(len(operands))
        ],
        out_specs=jax.tree.map(lambda _: pl.BlockSpec(memory_space=pltpu.VMEM), out_shape),
        compiler_params=pltpu.CompilerParams(vmem_limit_bytes=VMEM_BYTES),
    )(*operands)


def _fetched(value, rows, cols):
    lats, lons = lax.axis_size("lat"), lax.axis_size("lon")
    if not rows:
        return lax.ppermute(value, "lon", [((j + cols) % lons, j) for j in range(lons)])
    if not cols:
        return lax.ppermute(value, "lat", [((i + rows) % lats, i) for i in range(lats)])
    pairs = [
        (((i + rows) % lats) * lons + (j + cols) % lons, i * lons + j)
        for i in range(lats)
        for j in range(lons)
    ]
    return lax.ppermute(value, ("lat", "lon"), pairs)


def on_device(
    latent_field, gain_win, w_qkv_win, w_out_win, gain_shift, w_qkv_shift, w_out_shift,
    gain_mlp, w_up, w_down, gain_merge, w_merge,
):
    width = latent_field.shape[-1]
    quad = jax.ShapeDtypeStruct((QUAD, width), jnp.bfloat16)
    quads = _quadrant_tokens()
    plain = _window_tokens((0, 1, 2, 3))
    rolled = _window_tokens((1, 2, 3, 0))
    last = (lax.axis_index("lat") == lax.axis_size("lat") - 1).astype(jnp.int32).reshape(1, 1)

    x = latent_field.reshape(WLAT * WLON, LEV, width)
    to_win, to_quad = _permutation(plain, _natural_tokens()), _permutation(quads, plain)
    operands = (x, to_win, to_quad, gain_win.reshape(1, -1), w_qkv_win, w_out_win)
    held = (x, to_win, gain_win.reshape(1, -1), w_qkv_win, w_out_win, to_quad)
    nw, ne, sw, se = pl.pallas_call(
        window_kernel,
        out_shape=(quad,) * 4,
        in_specs=[pl.BlockSpec(memory_space=pltpu.HBM)] * len(operands),
        out_specs=(pl.BlockSpec(memory_space=pltpu.VMEM),) * 4,
        scratch_shapes=[pltpu.VMEM(array.shape, array.dtype) for array in held]
        + [pltpu.SemaphoreType.DMA((len(held),))],
        compiler_params=pltpu.CompilerParams(vmem_limit_bytes=VMEM_BYTES),
    )(*map(_in_hbm, operands))
    (
        shift_in, shift_out, to_merge, gain_shift, w_qkv_shift, w_out_shift,
        gain_mlp, w_up, w_down, gain_merge, w_merge,
    ) = _prefetched(
        nw,
        (
            _permutation(rolled, quads), _permutation(quads, rolled),
            _permutation(_merge_tokens(), quads), gain_shift.reshape(1, -1), w_qkv_shift,
            w_out_shift, gain_mlp.reshape(1, -1), w_up, w_down, gain_merge.reshape(1, -1), w_merge,
        ),
    )
    east = _fetched(sw, 0, 1)
    south = _fetched(ne, 1, 0)
    corner = _fetched(nw, 1, 1)
    own, to_east, to_south, to_corner = _call(
        shift_kernel,
        (
            last, se, east, south, corner, shift_in, shift_out, gain_shift, w_qkv_shift,
            w_out_shift,
        ),
        (quad,) * 4,
        smem=(0,),
    )
    b_sw = _fetched(to_east, 0, -1)
    b_ne = _fetched(to_south, -1, 0)
    b_nw = _fetched(to_corner, -1, -1)
    merged = _call(
        merge_kernel,
        (
            nw, ne, sw, se, b_nw, b_ne, b_sw, own, to_merge, gain_mlp, w_up, w_down, gain_merge,
            w_merge,
        ),
        jax.ShapeDtypeStruct((QUAD // LEV, LEV, 2 * width), jnp.bfloat16),
    )
    return merged.reshape(WLAT // 2, WLON // 2, LEV, 2 * width)


def solution(mesh):
    in_specs = (P("lat", "lon", None, None),) + (P(),) * 11
    return jax.shard_map(
        on_device,
        mesh=mesh,
        in_specs=in_specs,
        out_specs=P("lat", "lon", None, None),
        check_vma=False,
    )
```

```python
import math

import jax
import jax.numpy as jnp
import numpy as np
from jax import lax
from jax.experimental import pallas as pl
from jax.experimental.pallas import tpu as pltpu
from jax.sharding import PartitionSpec as P

HEADS = 16
HEAD = 32
WLAT = 6
WLON = 12
WLEV = 2
LEV = 4
HALF_LAT = WLAT // 2
HALF_LON = WLON // 2
WIN = WLAT * WLON * WLEV
TOKENS = WLAT * WLON * LEV
QUAD = TOKENS // 4
GROUP = 8
LANES = GROUP * HEAD
PIECE = QUAD // 2
PAD = 40
PQUAD = 2 * PAD
PTOKENS = 4 * PQUAD
KEYS = 4 * PAD
VMEM_BYTES = 28 * 1024 * 1024
MASKED = -1e30

epsilon = 1e-05


def _natural_tokens():
    return [(r, c, l) for r in range(WLAT) for c in range(WLON) for l in range(LEV)]


def _window_tokens():
    return [(r, c, l) for l in range(LEV) for r in range(WLAT) for c in range(WLON)]


def _quadrant_tokens(odd):
    sides = (0, 1) if odd else (1, 0)
    tokens = []
    for side in sides:
        for half in range(2):
            for pair in ((1, 2), (3, 0)):
                tokens += [
                    (half * HALF_LAT + r, side * HALF_LON + c, l)
                    for l in pair
                    for r in range(HALF_LAT)
                    for c in range(HALF_LON)
                ]
                tokens += [None] * (PAD - PIECE)
    return tokens


def _merge_tokens():
    return [
        (2 * i + piece % 2, 2 * j + piece // 2, l)
        for piece in range(4)
        for i in range(WLAT // 2)
        for j in range(WLON // 2)
        for l in range(LEV)
    ]


def _permutation(target, source):
    place = {token: index for index, token in enumerate(source)}
    matrix = np.zeros((len(target), len(source)), np.float32)
    for index, token in enumerate(target):
        if token is not None:
            matrix[index, place[token]] = 1.0
    return matrix


def _bias():
    within = np.arange(KEYS) % PAD
    query = np.arange(GROUP * PAD) % PAD
    filled = np.where(within >= PIECE, MASKED, 0.0)[:, None] + np.zeros((1, GROUP * PAD))
    apart = (within >= PIECE // 2)[:, None] != (query >= PIECE // 2)[None, :]
    return np.stack([filled, filled + np.where(apart, MASKED, 0.0)]).astype(np.float32)


def normed(values, gain_row):
    centered = values - jnp.mean(values, axis=-1, keepdims=True)
    spread = jnp.mean(centered * centered, axis=-1, keepdims=True)
    return centered * lax.rsqrt(spread + epsilon) * gain_row


def dot(left, right):
    return jnp.dot(left, right, preferred_element_type=jnp.float32)


def attend(windows):
    count = windows[0][0].shape[0]
    lane = lax.broadcasted_iota(jnp.int32, (count, LANES), 1)
    heads = [
        ((lane >= h * HEAD) & (lane < (h + 1) * HEAD)).astype(jnp.float32) for h in range(GROUP)
    ]
    heads = [head.astype(windows[0][0].dtype) for head in heads]
    scale = math.log2(math.e) / math.sqrt(HEAD)
    scores = []
    for query, key, _, bias in windows:
        stacked = jnp.concatenate([query * head for head in heads], axis=0).astype(jnp.bfloat16)
        score = lax.dot_general(
            key, stacked, (((1,), (1,)), ((), ())), preferred_element_type=jnp.float32
        )
        scores.append(score if bias is None else score + bias)
    probs = []
    for score in scores:
        weights = jnp.exp2((score - jnp.max(score, axis=0, keepdims=True)) * scale)
        total = jnp.sum(weights, axis=0, keepdims=True)
        probs.append((weights * (1.0 / total)).astype(jnp.bfloat16))
    mixed = [
        lax.dot_general(
            prob, window[2], (((0,), (0,)), ((), ())), preferred_element_type=jnp.float32
        )
        for prob, window in zip(probs, windows)
    ]
    contexts = []
    for mix in mixed:
        context = mix[:count]
        for h in range(1, GROUP):
            context = jnp.where(lane >= h * HEAD, mix[h * count : (h + 1) * count], context)
        contexts.append(context)
    return contexts


def by_rows(contexts):
    per = HEADS // GROUP
    return jnp.concatenate(
        [
            jnp.concatenate(contexts[start : start + per], axis=1)
            for start in range(0, len(contexts), per)
        ],
        axis=0,
    ).astype(jnp.bfloat16)


def _fetch(pairs, sems):
    copies = [
        pltpu.make_async_copy(source, target, sems.at[index])
        for index, (source, target) in enumerate(pairs)
    ]
    for copy in copies:
        copy.start()
    return copies


def window_kernel(
    x_hbm, to_win_hbm, gain_hbm, w_qkv_hbm, w_out_hbm, to_quad_hbm, gain_shift_hbm,
    w_next_hbm, kept_ref, north_ref, south_ref, w_next_ref,
    x_ref, to_win_ref, gain_ref, w_qkv_ref, w_out_ref, to_quad_ref, gain_shift_ref, sems,
):
    odd = lax.rem(lax.axis_index("lon"), 2)
    copies = _fetch(
        (
            (x_hbm, x_ref), (to_win_hbm, to_win_ref), (gain_hbm, gain_ref),
            (w_qkv_hbm, w_qkv_ref), (w_out_hbm, w_out_ref),
            (to_quad_hbm.at[odd], to_quad_ref), (gain_shift_hbm, gain_shift_ref),
            (w_next_hbm, w_next_ref),
        ),
        sems,
    )
    for copy in copies[:3]:
        copy.wait()
    width = x_ref.shape[-1]
    x = x_ref[...].astype(jnp.float32).reshape(TOKENS, width).astype(jnp.bfloat16)
    x = dot(to_win_ref[...], x)
    tokens = normed(x, gain_ref[...]).astype(jnp.bfloat16)
    copies[3].wait()
    query, key, value = (
        dot(tokens, w_qkv_ref[:, part * width : (part + 1) * width]).astype(jnp.bfloat16)
        for part in range(3)
    )
    windows = []
    for w in range(TOKENS // WIN):
        rows = slice(w * WIN, (w + 1) * WIN)
        for g in range(HEADS // GROUP):
            cols = slice(g * LANES, (g + 1) * LANES)
            windows.append((query[rows, cols], key[rows, cols], value[rows, cols], None))
    context = by_rows(attend(windows))
    for copy in copies[4:7]:
        copy.wait()
    after = (x + dot(context, w_out_ref[...])).astype(jnp.bfloat16)
    after = dot(to_quad_ref[...], after)
    kept_ref[...] = after.astype(jnp.bfloat16)
    quads = normed(after, gain_shift_ref[...]).astype(jnp.bfloat16)
    for half, ref in enumerate((north_ref, south_ref)):
        ref[:PQUAD] = quads[half * PQUAD : (half + 1) * PQUAD]
        ref[PQUAD:] = quads[(2 + half) * PQUAD : (3 + half) * PQUAD]
    copies[7].wait()


def own_kernel(
    north_ref, south_ref, w_qkv_ref, bias_hbm,
    query_ref, kv_ref, side_a_ref, side_b_ref, bias_ref, sems,
):
    copies = _fetch(((bias_hbm, bias_ref),), sems)
    side_a = jnp.concatenate([north_ref[:PQUAD], south_ref[:PQUAD]], axis=0)
    side_b = jnp.concatenate([north_ref[PQUAD:], south_ref[PQUAD:]], axis=0)
    side_a_ref[...] = side_a
    side_b_ref[...] = side_b
    tokens = jnp.concatenate([side_a, side_b], axis=0)
    width = tokens.shape[-1]
    query_ref[...] = dot(tokens, w_qkv_ref[:, :width])
    kv_ref[...] = dot(tokens, w_qkv_ref[:, width:])
    copies[0].wait()


def side_context(side, query_ref, kv_ref, kv_near_ref, kv_corner_ref, bias_ref):
    width = query_ref.shape[-1]
    band = lax.axis_index("lat")
    place = lax.broadcasted_iota(jnp.int32, (KEYS, GROUP * PAD), 0)
    across = ((place >= PAD) & (place < 2 * PAD)) | (place >= 3 * PAD)
    windows = []
    for half in range(2):
        edge = band == (0 if half == 0 else lax.axis_size("lat") - 1)
        seam = jnp.where(across & edge, jnp.float32(MASKED), jnp.float32(0.0))
        own = (side * 2 + half) * PQUAD
        for pair in range(2):
            bias = bias_ref[pair] + seam
            at = pair * PAD
            kv = jnp.concatenate(
                [
                    ref[start + at : start + at + PAD]
                    for ref, start in (
                        (kv_ref, own), (kv_near_ref, half * PQUAD),
                        (kv_near_ref, (2 + half) * PQUAD), (kv_corner_ref, half * PQUAD),
                    )
                ],
                axis=0,
            ).astype(jnp.bfloat16)
            query = query_ref[own + at : own + at + PAD]
            for g in range(HEADS // GROUP):
                cols = slice(g * LANES, (g + 1) * LANES)
                values = slice(width + g * LANES, width + (g + 1) * LANES)
                windows.append((query[:, cols], kv[:, cols], kv[:, values], bias))
    return by_rows(attend(windows))


def near_kernel(
    north_ref, south_ref, side_a_ref, side_b_ref, corner_ref, query_ref, kv_ref, w_qkv_ref,
    bias_ref, context_ref, kv_b_ref, kv_a_ref, kv_corner_ref,
):
    width = query_ref.shape[-1]
    w_kv = w_qkv_ref[:, width:]
    kv_a_ref[...] = dot(
        jnp.concatenate([north_ref[:PQUAD], south_ref[:PQUAD], side_a_ref[...]], axis=0), w_kv
    )
    kv_corner_ref[...] = dot(corner_ref[...], w_kv)
    kv_b_ref[...] = dot(
        jnp.concatenate([north_ref[PQUAD:], south_ref[PQUAD:], side_b_ref[...]], axis=0), w_kv
    )
    context_ref[...] = side_context(0, query_ref, kv_ref, kv_a_ref, kv_corner_ref, bias_ref)


def last_kernel(
    corner_ref, kept_ref, context_ref, query_ref, kv_ref, kv_b_ref, w_qkv_ref, bias_ref,
    w_out_hbm, gain_mlp_hbm, w_up_hbm, w_down_hbm, to_merge_hbm, gain_merge_hbm, w_merge_hbm,
    out_ref, kv_corner_ref,
    w_out_ref, gain_mlp_ref, w_up_ref, w_down_ref, to_merge_ref, gain_merge_ref, w_merge_ref, sems,
):
    odd = lax.rem(lax.axis_index("lon"), 2)
    copies = _fetch(
        (
            (w_out_hbm, w_out_ref), (gain_mlp_hbm, gain_mlp_ref), (w_up_hbm, w_up_ref),
            (w_down_hbm, w_down_ref), (to_merge_hbm.at[odd], to_merge_ref),
            (gain_merge_hbm, gain_merge_ref), (w_merge_hbm, w_merge_ref),
        ),
        sems,
    )
    width = kept_ref.shape[-1]
    kv_corner_ref[...] = dot(corner_ref[...], w_qkv_ref[:, width:])
    context = side_context(1, query_ref, kv_ref, kv_b_ref, kv_corner_ref, bias_ref)
    context = jnp.concatenate([context_ref[...], context], axis=0)
    copies[0].wait()
    branch = dot(context, w_out_ref[...]).astype(jnp.bfloat16).astype(jnp.float32)
    copies[1].wait()
    shift = (kept_ref[...].astype(jnp.float32) + branch).astype(jnp.bfloat16).astype(jnp.float32)
    tokens = normed(shift, gain_mlp_ref[...]).astype(jnp.bfloat16)
    copies[2].wait()
    hidden = jax.nn.gelu(dot(tokens, w_up_ref[...]), approximate=True).astype(jnp.bfloat16)
    copies[3].wait()
    after = (shift + dot(hidden, w_down_ref[...])).astype(jnp.bfloat16)
    copies[4].wait()
    merge = dot(to_merge_ref[...], after)
    stacked = jnp.concatenate([merge[i * QUAD : (i + 1) * QUAD] for i in range(4)], axis=1)
    copies[5].wait()
    tokens = normed(stacked, gain_merge_ref[...]).astype(jnp.bfloat16)
    copies[6].wait()
    merged = dot(tokens, w_merge_ref[...])
    out_ref[...] = merged.reshape(out_ref.shape).astype(jnp.bfloat16)


def _in_hbm(array):
    return pltpu.with_memory_space_constraint(array, pltpu.HBM)


def _call(kernel, near, far, outs, scratch=(), copies=0, flops=0):
    near_spec, far_spec = pl.BlockSpec(memory_space=pltpu.VMEM), pl.BlockSpec(memory_space=pltpu.HBM)
    return pl.pallas_call(
        kernel,
        out_shape=outs,
        in_specs=[near_spec] * len(near) + [far_spec] * len(far),
        out_specs=jax.tree.map(lambda _: near_spec, outs),
        scratch_shapes=list(scratch) + ([pltpu.SemaphoreType.DMA((copies,))] if copies else []),
        compiler_params=pltpu.CompilerParams(vmem_limit_bytes=VMEM_BYTES),
        cost_estimate=pl.CostEstimate(flops=flops, bytes_accessed=0, transcendentals=0),
    )(*near, *map(_in_hbm, far))


def _vmem(array):
    return pltpu.VMEM(array.shape, array.dtype)


def _rows(value, step):
    count = lax.axis_size("lat")
    return lax.ppermute(value, "lat", [((i + step) % count, i) for i in range(count)])


def _swap(value, first):
    count = lax.axis_size("lon")
    pairs = [(j % count, (j + 1) % count) for j in range(first, count + first, 2)]
    return lax.ppermute(value, "lon", pairs + [(b, a) for a, b in pairs])


def on_device(
    latent_field, gain_win, w_qkv_win, w_out_win, gain_shift, w_qkv_shift, w_out_shift,
    gain_mlp, w_up, w_down, gain_merge, w_merge,
):
    width = latent_field.shape[-1]
    natural, windows, merges = _natural_tokens(), _window_tokens(), _merge_tokens()
    quads = [_quadrant_tokens(odd) for odd in (False, True)]
    to_win = jnp.asarray(_permutation(windows, natural), jnp.bfloat16)
    to_quad = jnp.asarray(np.stack([_permutation(q, windows) for q in quads]), jnp.bfloat16)
    to_merge = jnp.asarray(np.stack([_permutation(merges, q) for q in quads]), jnp.bfloat16)
    bias = jnp.asarray(_bias())
    gain_win, gain_shift, gain_mlp, gain_merge = (
        gain.reshape(1, -1) for gain in (gain_win, gain_shift, gain_mlp, gain_merge)
    )

    def bf16(rows, cols=width):
        return pltpu.VMEM((rows, cols), jnp.bfloat16)

    def f32(rows, cols):
        return pltpu.VMEM((rows, cols), jnp.float32)

    x = latent_field.reshape(WLAT * WLON, LEV, width)
    first = (x, to_win, gain_win, w_qkv_win, w_out_win, to_quad, gain_shift, w_qkv_shift)
    held = [_vmem(array) for array in first[:-1]]
    held[5] = bf16(PTOKENS, TOKENS)
    kept, north, south, w_qkv = _call(
        window_kernel, (), first,
        (bf16(PTOKENS), bf16(2 * PQUAD), bf16(2 * PQUAD), _vmem(w_qkv_shift)), held, len(first),
    )
    from_north = _rows(south, -1)
    from_south = _rows(north, 1)
    query, kv, side_a, side_b, bias = _call(
        own_kernel, (north, south, w_qkv), (bias,),
        (
            f32(PTOKENS, width), f32(PTOKENS, 2 * width), bf16(2 * PQUAD), bf16(2 * PQUAD),
            _vmem(bias),
        ),
        copies=1,
    )
    from_a = _swap(side_a, 0)
    from_b = _swap(side_b, 1)
    corner_a = _swap(jnp.concatenate([from_north[:PQUAD], from_south[:PQUAD]], axis=0), 0)
    corner_b = _swap(jnp.concatenate([from_north[PQUAD:], from_south[PQUAD:]], axis=0), 1)
    context, kv_b = _call(
        near_kernel,
        (from_north, from_south, from_a, from_b, corner_a, query, kv, w_qkv, bias), (),
        (bf16(2 * PQUAD), f32(4 * PQUAD, 2 * width)),
        (f32(4 * PQUAD, 2 * width), f32(2 * PQUAD, 2 * width)), flops=10**11,
    )
    far = (w_out_shift, gain_mlp, w_up, w_down, to_merge, gain_merge, w_merge)
    held = [_vmem(array) for array in far]
    held[4] = bf16(TOKENS, PTOKENS)
    merged = _call(
        last_kernel, (corner_b, kept, context, query, kv, kv_b, w_qkv, bias), far,
        jax.ShapeDtypeStruct((QUAD // LEV, LEV, 2 * width), jnp.bfloat16),
        [f32(2 * PQUAD, 2 * width)] + held, len(far),
    )
    return merged.reshape(WLAT // 2, WLON // 2, LEV, 2 * width)


def solution(mesh):
    in_specs = (P("lat", "lon", None, None),) + (P(),) * 11
    return jax.shard_map(
        on_device,
        mesh=mesh,
        in_specs=in_specs,
        out_specs=P("lat", "lon", None, None),
        check_vma=False,
    )
```

```python
import math

import jax
import jax.numpy as jnp
import numpy as np
from jax import lax
from jax.experimental import pallas as pl
from jax.experimental.pallas import tpu as pltpu
from jax.sharding import PartitionSpec as P

HEADS = 16
HEAD = 32
WLAT = 6
WLON = 12
WLEV = 2
LEV = 4
HALF_LAT = WLAT // 2
HALF_LON = WLON // 2
WIN = WLAT * WLON * WLEV
TOKENS = WLAT * WLON * LEV
QUAD = TOKENS // 4
GROUP = 8
LANES = GROUP * HEAD
PIECE = QUAD // 2
SLOT = 40
KEYS = 4 * PIECE
HALF = 2 * QUAD
VMEM_BYTES = 28 * 1024 * 1024
MASKED = -1e30

epsilon = 1e-05


def _natural_tokens():
    return [(r, c, l) for r in range(WLAT) for c in range(WLON) for l in range(LEV)]


def _window_tokens():
    return [(r, c, l) for l in range(LEV) for r in range(WLAT) for c in range(WLON)]


def _quadrant_tokens(odd):
    sides = (0, 1) if odd else (1, 0)
    tokens = []
    for side in sides:
        for half in range(2):
            for pair in ((1, 2), (3, 0)):
                tokens += [
                    (half * HALF_LAT + r, side * HALF_LON + c, l)
                    for l in pair
                    for r in range(HALF_LAT)
                    for c in range(HALF_LON)
                ]
    return tokens


def _merge_tokens():
    return [
        (2 * i + piece % 2, 2 * j + piece // 2, l)
        for piece in range(4)
        for i in range(WLAT // 2)
        for j in range(WLON // 2)
        for l in range(LEV)
    ]


def _permutation(target, source):
    place = {token: index for index, token in enumerate(source)}
    matrix = np.zeros((len(target), len(source)), np.float32)
    for index, token in enumerate(target):
        matrix[index, place[token]] = 1.0
    return matrix


def _bias():
    key = np.arange(KEYS) % PIECE >= PIECE // 2
    query = np.arange(GROUP * SLOT) % SLOT >= PIECE // 2
    return np.where(key[:, None] != query[None, :], MASKED, 0.0).astype(np.float32)


def normed(values, gain_row):
    centered = values - jnp.mean(values, axis=-1, keepdims=True)
    spread = jnp.mean(centered * centered, axis=-1, keepdims=True)
    return centered * lax.rsqrt(spread + epsilon) * gain_row


def dot(left, right):
    return jnp.dot(left, right, preferred_element_type=jnp.float32)


def attend(windows):
    count = windows[0][0].shape[0]
    lane = lax.broadcasted_iota(jnp.int32, (count, LANES), 1)
    heads = [
        ((lane >= h * HEAD) & (lane < (h + 1) * HEAD)).astype(jnp.float32) for h in range(GROUP)
    ]
    heads = [head.astype(windows[0][0].dtype) for head in heads]
    scale = math.log2(math.e) / math.sqrt(HEAD)
    scores = []
    for query, key, _, bias in windows:
        stacked = jnp.concatenate([query * head for head in heads], axis=0).astype(jnp.bfloat16)
        score = lax.dot_general(
            key, stacked, (((1,), (1,)), ((), ())), preferred_element_type=jnp.float32
        )
        scores.append(score if bias is None else score + bias)
    probs = []
    for score in scores:
        weights = jnp.exp2((score - jnp.max(score, axis=0, keepdims=True)) * scale)
        total = jnp.sum(weights, axis=0, keepdims=True)
        probs.append((weights * (1.0 / total)).astype(jnp.bfloat16))
    mixed = [
        lax.dot_general(
            prob, window[2], (((0,), (0,)), ((), ())), preferred_element_type=jnp.float32
        )
        for prob, window in zip(probs, windows)
    ]
    contexts = []
    for mix in mixed:
        context = mix[:count]
        for h in range(1, GROUP):
            context = jnp.where(lane >= h * HEAD, mix[h * count : (h + 1) * count], context)
        contexts.append(context)
    return contexts


def by_rows(contexts, count):
    per = HEADS // GROUP
    return jnp.concatenate(
        [
            jnp.concatenate(contexts[start : start + per], axis=1)[:count]
            for start in range(0, len(contexts), per)
        ],
        axis=0,
    ).astype(jnp.bfloat16)


def halves(ref):
    values = ref[...].astype(jnp.float32)
    return values[:QUAD], values[QUAD:]


def rounded(*parts):
    return jnp.concatenate(parts, axis=0).astype(jnp.bfloat16)


def _fetch(pairs, sems):
    copies = [
        pltpu.make_async_copy(source, target, sems.at[index])
        for index, (source, target) in enumerate(pairs)
    ]
    for copy in copies:
        copy.start()
    return copies


def window_kernel(
    x_hbm, to_win_hbm, gain_hbm, w_qkv_hbm, w_out_hbm, to_quad_hbm, gain_shift_hbm,
    w_next_hbm, kept_ref, north_ref, south_ref, w_next_ref,
    x_ref, to_win_ref, gain_ref, w_qkv_ref, w_out_ref, to_quad_ref, gain_shift_ref, sems,
):
    odd = lax.rem(lax.axis_index("lon"), 2)
    copies = _fetch(
        (
            (x_hbm, x_ref), (to_win_hbm, to_win_ref), (gain_hbm, gain_ref),
            (w_qkv_hbm, w_qkv_ref), (w_out_hbm, w_out_ref),
            (to_quad_hbm.at[odd], to_quad_ref), (gain_shift_hbm, gain_shift_ref),
            (w_next_hbm, w_next_ref),
        ),
        sems,
    )
    for copy in copies[:3]:
        copy.wait()
    width = x_ref.shape[-1]
    x = x_ref[...].astype(jnp.float32).reshape(TOKENS, width).astype(jnp.bfloat16)
    x = dot(to_win_ref[...], x)
    tokens = normed(x, gain_ref[...]).astype(jnp.bfloat16)
    copies[3].wait()
    query, key, value = (
        dot(tokens, w_qkv_ref[:, part * width : (part + 1) * width]).astype(jnp.bfloat16)
        for part in range(3)
    )
    windows = []
    for w in range(TOKENS // WIN):
        rows = slice(w * WIN, (w + 1) * WIN)
        for g in range(HEADS // GROUP):
            cols = slice(g * LANES, (g + 1) * LANES)
            windows.append((query[rows, cols], key[rows, cols], value[rows, cols], None))
    context = by_rows(attend(windows), WIN)
    for copy in copies[4:7]:
        copy.wait()
    after = (x + dot(context, w_out_ref[...])).astype(jnp.bfloat16)
    after = dot(to_quad_ref[...], after)
    kept_ref[...] = after.astype(jnp.bfloat16)
    quads = normed(after, gain_shift_ref[...])
    for half, ref in enumerate((north_ref, south_ref)):
        ref[...] = rounded(
            *(quads[start : start + QUAD] for start in (half * QUAD, HALF + half * QUAD))
        )
    copies[7].wait()


def own_kernel(
    north_ref, south_ref, w_qkv_ref, bias_hbm,
    query_ref, kv_ref, side_a_ref, side_b_ref, bias_ref, sems,
):
    copies = _fetch(((bias_hbm, bias_ref),), sems)
    (na, nb), (sa, sb) = halves(north_ref), halves(south_ref)
    side_a, side_b = rounded(na, sa), rounded(nb, sb)
    side_a_ref[...] = side_a
    side_b_ref[...] = side_b
    tokens = jnp.concatenate([side_a, side_b], axis=0)
    width = tokens.shape[-1]
    query_ref[:TOKENS] = dot(tokens, w_qkv_ref[:, :width])
    query_ref[TOKENS:] = jnp.zeros_like(query_ref[TOKENS:])
    kv_ref[...] = dot(tokens, w_qkv_ref[:, width:])
    copies[0].wait()


def side_context(side, query_ref, kv_ref, kv_near_ref, kv_corner_ref, bias_ref):
    width = query_ref.shape[-1]
    band = lax.axis_index("lat")
    place = lax.broadcasted_iota(jnp.int32, (KEYS, GROUP * SLOT), 0)
    across = ((place >= PIECE) & (place < 2 * PIECE)) | (place >= 3 * PIECE)
    windows = []
    for half in range(2):
        edge = band == (0 if half == 0 else lax.axis_size("lat") - 1)
        seam = jnp.where(across & edge, jnp.float32(MASKED), jnp.float32(0.0))
        own = side * HALF + half * QUAD
        for pair in range(2):
            bias = seam if pair == 0 else seam + bias_ref[...]
            at = pair * PIECE
            kv = rounded(
                *(
                    ref[start + at : start + at + PIECE]
                    for ref, start in (
                        (kv_ref, own), (kv_near_ref, half * QUAD),
                        (kv_near_ref, HALF + half * QUAD), (kv_corner_ref, half * QUAD),
                    )
                )
            )
            query = query_ref[own + at : own + at + SLOT]
            for g in range(HEADS // GROUP):
                cols = slice(g * LANES, (g + 1) * LANES)
                values = slice(width + g * LANES, width + (g + 1) * LANES)
                windows.append((query[:, cols], kv[:, cols], kv[:, values], bias))
    return by_rows(attend(windows), PIECE)


def block(context, kept, w_out, gain_mlp, w_up, w_down):
    branch = dot(context, w_out()).astype(jnp.bfloat16).astype(jnp.float32)
    shift = (kept.astype(jnp.float32) + branch).astype(jnp.bfloat16).astype(jnp.float32)
    tokens = normed(shift, gain_mlp()).astype(jnp.bfloat16)
    hidden = jax.nn.gelu(dot(tokens, w_up()), approximate=True).astype(jnp.bfloat16)
    return (shift + dot(hidden, w_down())).astype(jnp.bfloat16)


def near_kernel(
    north_ref, south_ref, side_a_ref, side_b_ref, corner_ref, kept_ref, query_ref, kv_ref,
    w_qkv_ref, bias_ref, w_out_hbm, gain_mlp_hbm, w_up_hbm, w_down_hbm,
    after_ref, kv_b_ref, w_out_ref, gain_mlp_ref, w_up_ref, w_down_ref,
    kv_a_ref, kv_corner_ref, sems,
):
    pairs = (
        (w_out_hbm, w_out_ref), (gain_mlp_hbm, gain_mlp_ref), (w_up_hbm, w_up_ref),
        (w_down_hbm, w_down_ref),
    )
    copies = _fetch(pairs, sems)

    def arrived(index):
        def array():
            copies[index].wait()
            return pairs[index][1][...]

        return array

    width = query_ref.shape[-1]
    w_kv = w_qkv_ref[:, width:]
    (north_a, north_b), (south_a, south_b) = halves(north_ref), halves(south_ref)
    kv_a_ref[:HALF] = dot(rounded(north_a, south_a), w_kv)
    kv_a_ref[HALF:] = dot(side_a_ref[...], w_kv)
    kv_corner_ref[...] = dot(corner_ref[...], w_kv)
    kv_b_ref[:HALF] = dot(rounded(north_b, south_b), w_kv)
    kv_b_ref[HALF:] = dot(side_b_ref[...], w_kv)
    context = side_context(0, query_ref, kv_ref, kv_a_ref, kv_corner_ref, bias_ref)
    after_ref[...] = block(context, kept_ref[:HALF], *map(arrived, range(4)))


def last_kernel(
    corner_ref, kept_ref, after_ref, query_ref, kv_ref, kv_b_ref, w_qkv_ref, bias_ref,
    w_out_ref, gain_mlp_ref, w_up_ref, w_down_ref, to_merge_hbm, gain_merge_hbm, w_merge_hbm,
    out_ref, kv_corner_ref, to_merge_ref, gain_merge_ref, w_merge_ref, sems,
):
    odd = lax.rem(lax.axis_index("lon"), 2)
    copies = _fetch(
        (
            (to_merge_hbm.at[odd], to_merge_ref), (gain_merge_hbm, gain_merge_ref),
            (w_merge_hbm, w_merge_ref),
        ),
        sems,
    )
    width = kept_ref.shape[-1]
    kv_corner_ref[...] = dot(corner_ref[...], w_qkv_ref[:, width:])
    context = side_context(1, query_ref, kv_ref, kv_b_ref, kv_corner_ref, bias_ref)
    weights = (w_out_ref, gain_mlp_ref, w_up_ref, w_down_ref)
    after = block(
        context, kept_ref[HALF:], *(lambda ref=ref: ref[...] for ref in weights)
    )
    copies[0].wait()
    merge = dot(to_merge_ref[...], jnp.concatenate([after_ref[...], after], axis=0))
    stacked = jnp.concatenate([merge[i * QUAD : (i + 1) * QUAD] for i in range(4)], axis=1)
    copies[1].wait()
    tokens = normed(stacked, gain_merge_ref[...]).astype(jnp.bfloat16)
    copies[2].wait()
    merged = dot(tokens, w_merge_ref[...])
    out_ref[...] = merged.reshape(out_ref.shape).astype(jnp.bfloat16)


def _in_hbm(array):
    return pltpu.with_memory_space_constraint(array, pltpu.HBM)


def _call(kernel, near, far, outs, scratch=(), copies=0, flops=0):
    near_spec, far_spec = pl.BlockSpec(memory_space=pltpu.VMEM), pl.BlockSpec(memory_space=pltpu.HBM)
    return pl.pallas_call(
        kernel,
        out_shape=outs,
        in_specs=[near_spec] * len(near) + [far_spec] * len(far),
        out_specs=jax.tree.map(lambda _: near_spec, outs),
        scratch_shapes=list(scratch) + ([pltpu.SemaphoreType.DMA((copies,))] if copies else []),
        compiler_params=pltpu.CompilerParams(vmem_limit_bytes=VMEM_BYTES),
        cost_estimate=pl.CostEstimate(flops=flops, bytes_accessed=0, transcendentals=0),
    )(*near, *map(_in_hbm, far))


def _vmem(array):
    return pltpu.VMEM(array.shape, array.dtype)


def _rows(value, step):
    count = lax.axis_size("lat")
    return lax.ppermute(value, "lat", [((i + step) % count, i) for i in range(count)])


def _swap(value, first):
    count = lax.axis_size("lon")
    pairs = [(j % count, (j + 1) % count) for j in range(first, count + first, 2)]
    return lax.ppermute(value, "lon", pairs + [(b, a) for a, b in pairs])


def on_device(
    latent_field, gain_win, w_qkv_win, w_out_win, gain_shift, w_qkv_shift, w_out_shift,
    gain_mlp, w_up, w_down, gain_merge, w_merge,
):
    width = latent_field.shape[-1]
    natural, windows, merges = _natural_tokens(), _window_tokens(), _merge_tokens()
    quads = [_quadrant_tokens(odd) for odd in (False, True)]
    to_win = jnp.asarray(_permutation(windows, natural), jnp.bfloat16)
    to_quad = jnp.asarray(np.stack([_permutation(q, windows) for q in quads]), jnp.bfloat16)
    to_merge = jnp.asarray(np.stack([_permutation(merges, q) for q in quads]), jnp.bfloat16)
    bias = jnp.asarray(_bias())
    gain_win, gain_shift, gain_mlp, gain_merge = (
        gain.reshape(1, -1) for gain in (gain_win, gain_shift, gain_mlp, gain_merge)
    )

    def bf16(rows, cols=width):
        return pltpu.VMEM((rows, cols), jnp.bfloat16)

    def f32(rows, cols):
        return pltpu.VMEM((rows, cols), jnp.float32)

    x = latent_field.reshape(WLAT * WLON, LEV, width)
    first = (x, to_win, gain_win, w_qkv_win, w_out_win, to_quad, gain_shift, w_qkv_shift)
    held = [_vmem(array) for array in first[:-1]]
    held[5] = bf16(TOKENS, TOKENS)
    kept, north, south, w_qkv = _call(
        window_kernel, (), first,
        (bf16(TOKENS), bf16(HALF), bf16(HALF), _vmem(w_qkv_shift)), held, len(first),
    )
    from_north = _rows(south, -1)
    from_south = _rows(north, 1)
    query, kv, side_a, side_b, bias = _call(
        own_kernel, (north, south, w_qkv), (bias,),
        (
            f32(TOKENS + 8, width), f32(TOKENS, 2 * width), bf16(HALF), bf16(HALF),
            _vmem(bias),
        ),
        copies=1,
    )
    from_a = _swap(side_a, 0)
    from_b = _swap(side_b, 1)
    corner_a = _swap(jnp.concatenate([from_north[:QUAD], from_south[:QUAD]], axis=0), 0)
    corner_b = _swap(jnp.concatenate([from_north[QUAD:], from_south[QUAD:]], axis=0), 1)
    far = (w_out_shift, gain_mlp, w_up, w_down)
    after, kv_b, *weights = _call(
        near_kernel,
        (from_north, from_south, from_a, from_b, corner_a, kept, query, kv, w_qkv, bias), far,
        (bf16(HALF), f32(TOKENS, 2 * width), *map(_vmem, far)),
        (f32(TOKENS, 2 * width), f32(HALF, 2 * width)), len(far), flops=10**11,
    )
    merged = _call(
        last_kernel, (corner_b, kept, after, query, kv, kv_b, w_qkv, bias, *weights),
        (to_merge, gain_merge, w_merge),
        jax.ShapeDtypeStruct((QUAD // LEV, LEV, 2 * width), jnp.bfloat16),
        (
            f32(HALF, 2 * width), bf16(TOKENS, TOKENS), _vmem(gain_merge), _vmem(w_merge),
        ),
        3,
    )
    return merged.reshape(WLAT // 2, WLON // 2, LEV, 2 * width)


def solution(mesh):
    in_specs = (P("lat", "lon", None, None),) + (P(),) * 11
    return jax.shard_map(
        on_device,
        mesh=mesh,
        in_specs=in_specs,
        out_specs=P("lat", "lon", None, None),
        check_vma=False,
    )
```

```python
import math

import jax
import jax.numpy as jnp
import numpy as np
from jax import lax
from jax.experimental import pallas as pl
from jax.experimental.pallas import tpu as pltpu
from jax.sharding import PartitionSpec as P

HEADS = 16
HEAD = 32
WLAT = 6
WLON = 12
WLEV = 2
LEV = 4
HALF_LAT = WLAT // 2
HALF_LON = WLON // 2
WIN = WLAT * WLON * WLEV
TOKENS = WLAT * WLON * LEV
QUAD = TOKENS // 4
GROUP = 8
LANES = GROUP * HEAD
PIECE = QUAD // 2
SLOT = 40
KEYS = 4 * PIECE
HALF = 2 * QUAD
VMEM_BYTES = 28 * 1024 * 1024
MASKED = -1e30

epsilon = 1e-05


def _natural_tokens():
    return [(r, c, l) for r in range(WLAT) for c in range(WLON) for l in range(LEV)]


def _window_tokens():
    return [(r, c, l) for l in range(LEV) for r in range(WLAT) for c in range(WLON)]


def _quadrant_tokens(odd):
    sides = (0, 1) if odd else (1, 0)
    tokens = []
    for side in sides:
        for half in range(2):
            for pair in ((1, 2), (3, 0)):
                tokens += [
                    (half * HALF_LAT + r, side * HALF_LON + c, l)
                    for l in pair
                    for r in range(HALF_LAT)
                    for c in range(HALF_LON)
                ]
    return tokens


def _merge_tokens():
    return [
        (2 * i + piece % 2, 2 * j + piece // 2, l)
        for piece in range(4)
        for i in range(WLAT // 2)
        for j in range(WLON // 2)
        for l in range(LEV)
    ]


def _permutation(target, source):
    place = {token: index for index, token in enumerate(source)}
    matrix = np.zeros((len(target), len(source)), np.float32)
    for index, token in enumerate(target):
        matrix[index, place[token]] = 1.0
    return matrix


def _bias():
    key = np.arange(KEYS) % PIECE >= PIECE // 2
    query = np.arange(GROUP * SLOT) % SLOT >= PIECE // 2
    return np.where(key[:, None] != query[None, :], MASKED, 0.0).astype(np.float32)


def normed(values, gain_row):
    centered = values - jnp.mean(values, axis=-1, keepdims=True)
    spread = jnp.mean(centered * centered, axis=-1, keepdims=True)
    return centered * lax.rsqrt(spread + epsilon) * gain_row


def dot(left, right):
    return jnp.dot(left, right, preferred_element_type=jnp.float32)


def attend(windows):
    count = windows[0][0].shape[0]
    lane = lax.broadcasted_iota(jnp.int32, (count, LANES), 1)
    heads = [
        ((lane >= h * HEAD) & (lane < (h + 1) * HEAD)).astype(jnp.float32) for h in range(GROUP)
    ]
    heads = [head.astype(windows[0][0].dtype) for head in heads]
    scale = math.log2(math.e) / math.sqrt(HEAD)
    scores = []
    for query, key, _, bias in windows:
        stacked = jnp.concatenate([query * head for head in heads], axis=0).astype(jnp.bfloat16)
        score = lax.dot_general(
            key, stacked, (((1,), (1,)), ((), ())), preferred_element_type=jnp.float32
        )
        scores.append(score if bias is None else score + bias)
    probs = []
    for score in scores:
        weights = jnp.exp2((score - jnp.max(score, axis=0, keepdims=True)) * scale)
        total = jnp.sum(weights, axis=0, keepdims=True)
        probs.append((weights * (1.0 / total)).astype(jnp.bfloat16))
    mixed = [
        lax.dot_general(
            prob, window[2], (((0,), (0,)), ((), ())), preferred_element_type=jnp.float32
        )
        for prob, window in zip(probs, windows)
    ]
    contexts = []
    for mix in mixed:
        context = mix[:count]
        for h in range(1, GROUP):
            context = jnp.where(lane >= h * HEAD, mix[h * count : (h + 1) * count], context)
        contexts.append(context)
    return contexts


def by_rows(contexts, count):
    per = HEADS // GROUP
    return jnp.concatenate(
        [
            jnp.concatenate(contexts[start : start + per], axis=1)[:count]
            for start in range(0, len(contexts), per)
        ],
        axis=0,
    ).astype(jnp.bfloat16)


def stage(body):
    pl.when(lax.axis_index("lat") >= 0)(body)


def halves(ref):
    values = ref[...].astype(jnp.float32)
    return values[:QUAD], values[QUAD:]


def rounded(*parts):
    return jnp.concatenate(parts, axis=0).astype(jnp.bfloat16)


def _fetch(pairs, sems):
    copies = [
        pltpu.make_async_copy(source, target, sems.at[index])
        for index, (source, target) in enumerate(pairs)
    ]
    for copy in copies:
        copy.start()
    return copies


def window_kernel(
    x_hbm, to_win_hbm, gain_hbm, w_qkv_hbm, w_out_hbm, to_quad_hbm, gain_shift_hbm,
    w_next_hbm, kept_ref, north_ref, south_ref, w_next_ref,
    x_ref, to_win_ref, gain_ref, w_qkv_ref, w_out_ref, to_quad_ref, gain_shift_ref, sems,
):
    odd = lax.rem(lax.axis_index("lon"), 2)
    copies = _fetch(
        (
            (x_hbm, x_ref), (to_win_hbm, to_win_ref), (gain_hbm, gain_ref),
            (w_qkv_hbm, w_qkv_ref), (w_out_hbm, w_out_ref),
            (to_quad_hbm.at[odd], to_quad_ref), (gain_shift_hbm, gain_shift_ref),
            (w_next_hbm, w_next_ref),
        ),
        sems,
    )
    for copy in copies[:3]:
        copy.wait()
    width = x_ref.shape[-1]
    x = x_ref[...].astype(jnp.float32).reshape(TOKENS, width).astype(jnp.bfloat16)
    x = dot(to_win_ref[...], x)
    tokens = normed(x, gain_ref[...]).astype(jnp.bfloat16)
    copies[3].wait()
    query, key, value = (
        dot(tokens, w_qkv_ref[:, part * width : (part + 1) * width]).astype(jnp.bfloat16)
        for part in range(3)
    )
    windows = []
    for w in range(TOKENS // WIN):
        rows = slice(w * WIN, (w + 1) * WIN)
        for g in range(HEADS // GROUP):
            cols = slice(g * LANES, (g + 1) * LANES)
            windows.append((query[rows, cols], key[rows, cols], value[rows, cols], None))
    context = by_rows(attend(windows), WIN)
    for copy in copies[4:7]:
        copy.wait()
    after = (x + dot(context, w_out_ref[...])).astype(jnp.bfloat16)
    after = dot(to_quad_ref[...], after)
    kept_ref[...] = after.astype(jnp.bfloat16)
    quads = normed(after, gain_shift_ref[...])
    for half, ref in enumerate((north_ref, south_ref)):
        ref[...] = rounded(
            *(quads[start : start + QUAD] for start in (half * QUAD, HALF + half * QUAD))
        )
    copies[7].wait()


def own_kernel(
    north_ref, south_ref, w_qkv_ref, bias_hbm,
    query_ref, kv_ref, side_a_ref, side_b_ref, bias_ref, sems,
):
    copies = _fetch(((bias_hbm, bias_ref),), sems)
    (na, nb), (sa, sb) = halves(north_ref), halves(south_ref)
    side_a, side_b = rounded(na, sa), rounded(nb, sb)
    side_a_ref[...] = side_a
    side_b_ref[...] = side_b
    tokens = jnp.concatenate([side_a, side_b], axis=0)
    width = tokens.shape[-1]
    query_ref[:TOKENS] = dot(tokens, w_qkv_ref[:, :width])
    query_ref[TOKENS:] = jnp.zeros_like(query_ref[TOKENS:])
    kv_ref[...] = dot(tokens, w_qkv_ref[:, width:])
    copies[0].wait()


def side_context(side, query_ref, kv_ref, kv_near_ref, kv_corner_ref, bias_ref):
    width = query_ref.shape[-1]
    band = lax.axis_index("lat")
    place = lax.broadcasted_iota(jnp.int32, (KEYS, GROUP * SLOT), 0)
    across = ((place >= PIECE) & (place < 2 * PIECE)) | (place >= 3 * PIECE)
    windows = []
    for half in range(2):
        edge = band == (0 if half == 0 else lax.axis_size("lat") - 1)
        seam = jnp.where(across & edge, jnp.float32(MASKED), jnp.float32(0.0))
        own = side * HALF + half * QUAD
        for pair in range(2):
            bias = seam if pair == 0 else seam + bias_ref[...]
            at = pair * PIECE
            kv = rounded(
                *(
                    ref[start + at : start + at + PIECE]
                    for ref, start in (
                        (kv_ref, own), (kv_near_ref, half * QUAD),
                        (kv_near_ref, HALF + half * QUAD), (kv_corner_ref, half * QUAD),
                    )
                )
            )
            query = query_ref[own + at : own + at + SLOT]
            for g in range(HEADS // GROUP):
                cols = slice(g * LANES, (g + 1) * LANES)
                values = slice(width + g * LANES, width + (g + 1) * LANES)
                windows.append((query[:, cols], kv[:, cols], kv[:, values], bias))
    return by_rows(attend(windows), PIECE)


def block(context, kept, w_out, gain_mlp, w_up, w_down):
    branch = dot(context, w_out()).astype(jnp.bfloat16).astype(jnp.float32)
    shift = (kept.astype(jnp.float32) + branch).astype(jnp.bfloat16).astype(jnp.float32)
    tokens = normed(shift, gain_mlp()).astype(jnp.bfloat16)
    hidden = jax.nn.gelu(dot(tokens, w_up()), approximate=True).astype(jnp.bfloat16)
    return (shift + dot(hidden, w_down())).astype(jnp.bfloat16)


def near_kernel(
    north_ref, south_ref, side_a_ref, side_b_ref, corner_ref, kept_ref, query_ref, kv_ref,
    w_qkv_ref, bias_ref, w_out_hbm, gain_mlp_hbm, w_up_hbm, w_down_hbm,
    after_ref, kv_b_ref, w_out_ref, gain_mlp_ref, w_up_ref, w_down_ref,
    kv_a_ref, kv_corner_ref, context_ref, sems,
):
    pairs = (
        (w_out_hbm, w_out_ref), (gain_mlp_hbm, gain_mlp_ref), (w_up_hbm, w_up_ref),
        (w_down_hbm, w_down_ref),
    )
    copies = _fetch(pairs, sems)

    def arrived(index):
        def array():
            copies[index].wait()
            return pairs[index][1][...]

        return array

    width = query_ref.shape[-1]

    @stage
    def _():
        (north_a, north_b), (south_a, south_b) = halves(north_ref), halves(south_ref)
        w_kv = w_qkv_ref[:, width:]
        kv_a_ref[:HALF] = dot(rounded(north_a, south_a), w_kv)
        kv_a_ref[HALF:] = dot(side_a_ref[...], w_kv)
        kv_corner_ref[...] = dot(corner_ref[...], w_kv)
        kv_b_ref[:HALF] = dot(rounded(north_b, south_b), w_kv)
        kv_b_ref[HALF:] = dot(side_b_ref[...], w_kv)

    @stage
    def _():
        context_ref[...] = side_context(0, query_ref, kv_ref, kv_a_ref, kv_corner_ref, bias_ref)

    after_ref[...] = block(context_ref[...], kept_ref[:HALF], *map(arrived, range(4)))


def last_kernel(
    corner_ref, kept_ref, after_ref, query_ref, kv_ref, kv_b_ref, w_qkv_ref, bias_ref,
    w_out_ref, gain_mlp_ref, w_up_ref, w_down_ref, to_merge_hbm, gain_merge_hbm, w_merge_hbm,
    out_ref, kv_corner_ref, context_ref, to_merge_ref, gain_merge_ref, w_merge_ref, sems,
):
    odd = lax.rem(lax.axis_index("lon"), 2)
    copies = _fetch(
        (
            (to_merge_hbm.at[odd], to_merge_ref), (gain_merge_hbm, gain_merge_ref),
            (w_merge_hbm, w_merge_ref),
        ),
        sems,
    )
    width = kept_ref.shape[-1]

    @stage
    def _():
        kv_corner_ref[...] = dot(corner_ref[...], w_qkv_ref[:, width:])

    @stage
    def _():
        context_ref[...] = side_context(1, query_ref, kv_ref, kv_b_ref, kv_corner_ref, bias_ref)

    weights = (w_out_ref, gain_mlp_ref, w_up_ref, w_down_ref)
    after = block(
        context_ref[...], kept_ref[HALF:], *(lambda ref=ref: ref[...] for ref in weights)
    )
    copies[0].wait()
    merge = dot(to_merge_ref[...], jnp.concatenate([after_ref[...], after], axis=0))
    stacked = jnp.concatenate([merge[i * QUAD : (i + 1) * QUAD] for i in range(4)], axis=1)
    copies[1].wait()
    tokens = normed(stacked, gain_merge_ref[...]).astype(jnp.bfloat16)
    copies[2].wait()
    merged = dot(tokens, w_merge_ref[...])
    out_ref[...] = merged.reshape(out_ref.shape).astype(jnp.bfloat16)


def _in_hbm(array):
    return pltpu.with_memory_space_constraint(array, pltpu.HBM)


def _call(kernel, near, far, outs, scratch=(), copies=0, flops=0):
    near_spec, far_spec = pl.BlockSpec(memory_space=pltpu.VMEM), pl.BlockSpec(memory_space=pltpu.HBM)
    return pl.pallas_call(
        kernel,
        out_shape=outs,
        in_specs=[near_spec] * len(near) + [far_spec] * len(far),
        out_specs=jax.tree.map(lambda _: near_spec, outs),
        scratch_shapes=list(scratch) + ([pltpu.SemaphoreType.DMA((copies,))] if copies else []),
        compiler_params=pltpu.CompilerParams(vmem_limit_bytes=VMEM_BYTES),
        cost_estimate=pl.CostEstimate(flops=flops, bytes_accessed=0, transcendentals=0),
    )(*near, *map(_in_hbm, far))


def _vmem(array):
    return pltpu.VMEM(array.shape, array.dtype)


def _rows(value, step):
    count = lax.axis_size("lat")
    return lax.ppermute(value, "lat", [((i + step) % count, i) for i in range(count)])


def _swap(value, first):
    count = lax.axis_size("lon")
    pairs = [(j % count, (j + 1) % count) for j in range(first, count + first, 2)]
    return lax.ppermute(value, "lon", pairs + [(b, a) for a, b in pairs])


def on_device(
    latent_field, gain_win, w_qkv_win, w_out_win, gain_shift, w_qkv_shift, w_out_shift,
    gain_mlp, w_up, w_down, gain_merge, w_merge,
):
    width = latent_field.shape[-1]
    natural, windows, merges = _natural_tokens(), _window_tokens(), _merge_tokens()
    quads = [_quadrant_tokens(odd) for odd in (False, True)]
    to_win = jnp.asarray(_permutation(windows, natural), jnp.bfloat16)
    to_quad = jnp.asarray(np.stack([_permutation(q, windows) for q in quads]), jnp.bfloat16)
    to_merge = jnp.asarray(np.stack([_permutation(merges, q) for q in quads]), jnp.bfloat16)
    bias = jnp.asarray(_bias())
    gain_win, gain_shift, gain_mlp, gain_merge = (
        gain.reshape(1, -1) for gain in (gain_win, gain_shift, gain_mlp, gain_merge)
    )

    def bf16(rows, cols=width):
        return pltpu.VMEM((rows, cols), jnp.bfloat16)

    def f32(rows, cols):
        return pltpu.VMEM((rows, cols), jnp.float32)

    x = latent_field.reshape(WLAT * WLON, LEV, width)
    first = (x, to_win, gain_win, w_qkv_win, w_out_win, to_quad, gain_shift, w_qkv_shift)
    held = [_vmem(array) for array in first[:-1]]
    held[5] = bf16(TOKENS, TOKENS)
    kept, north, south, w_qkv = _call(
        window_kernel, (), first,
        (bf16(TOKENS), bf16(HALF), bf16(HALF), _vmem(w_qkv_shift)), held, len(first),
    )
    from_north = _rows(south, -1)
    from_south = _rows(north, 1)
    query, kv, side_a, side_b, bias = _call(
        own_kernel, (north, south, w_qkv), (bias,),
        (
            f32(TOKENS + 8, width), f32(TOKENS, 2 * width), bf16(HALF), bf16(HALF),
            _vmem(bias),
        ),
        copies=1,
    )
    from_a = _swap(side_a, 0)
    from_b = _swap(side_b, 1)
    corner_a = _swap(jnp.concatenate([from_north[:QUAD], from_south[:QUAD]], axis=0), 0)
    corner_b = _swap(jnp.concatenate([from_north[QUAD:], from_south[QUAD:]], axis=0), 1)
    far = (w_out_shift, gain_mlp, w_up, w_down)
    after, kv_b, *weights = _call(
        near_kernel,
        (from_north, from_south, from_a, from_b, corner_a, kept, query, kv, w_qkv, bias), far,
        (bf16(HALF), f32(TOKENS, 2 * width), *map(_vmem, far)),
        (f32(TOKENS, 2 * width), f32(HALF, 2 * width), bf16(HALF)), len(far), flops=10**11,
    )
    merged = _call(
        last_kernel, (corner_b, kept, after, query, kv, kv_b, w_qkv, bias, *weights),
        (to_merge, gain_merge, w_merge),
        jax.ShapeDtypeStruct((QUAD // LEV, LEV, 2 * width), jnp.bfloat16),
        (
            f32(HALF, 2 * width), bf16(HALF), bf16(TOKENS, TOKENS), _vmem(gain_merge), _vmem(w_merge),
        ),
        3,
    )
    return merged.reshape(WLAT // 2, WLON // 2, LEV, 2 * width)


def solution(mesh):
    in_specs = (P("lat", "lon", None, None),) + (P(),) * 11
    return jax.shard_map(
        on_device,
        mesh=mesh,
        in_specs=in_specs,
        out_specs=P("lat", "lon", None, None),
        check_vma=False,
    )
```

```python
import math

import jax
import jax.numpy as jnp
import numpy as np
from jax import lax
from jax.experimental import pallas as pl
from jax.experimental.pallas import tpu as pltpu
from jax.sharding import PartitionSpec as P

HEADS = 16
HEAD = 32
WLAT = 6
WLON = 12
WLEV = 2
LEV = 4
HALF_LAT = WLAT // 2
HALF_LON = WLON // 2
WIN = WLAT * WLON * WLEV
TOKENS = WLAT * WLON * LEV
QUAD = TOKENS // 4
GROUP = 8
LANES = GROUP * HEAD
PIECE = QUAD // 2
SLOT = 40
KEYS = 4 * PIECE
HALF = 2 * QUAD
VMEM_BYTES = 28 * 1024 * 1024
MASKED = -1e30

epsilon = 1e-05


def _natural_tokens():
    return [(r, c, l) for r in range(WLAT) for c in range(WLON) for l in range(LEV)]


def _window_tokens():
    return [(r, c, l) for l in range(LEV) for r in range(WLAT) for c in range(WLON)]


def _quadrant_tokens(odd):
    sides = (0, 1) if odd else (1, 0)
    tokens = []
    for side in sides:
        for half in range(2):
            for pair in ((1, 2), (3, 0)):
                tokens += [
                    (half * HALF_LAT + r, side * HALF_LON + c, l)
                    for l in pair
                    for r in range(HALF_LAT)
                    for c in range(HALF_LON)
                ]
    return tokens


def _merge_tokens():
    return [
        (2 * i + piece % 2, 2 * j + piece // 2, l)
        for piece in range(4)
        for i in range(WLAT // 2)
        for j in range(WLON // 2)
        for l in range(LEV)
    ]


def _permutation(target, source):
    place = {token: index for index, token in enumerate(source)}
    matrix = np.zeros((len(target), len(source)), np.float32)
    for index, token in enumerate(target):
        matrix[index, place[token]] = 1.0
    return matrix


def _bias():
    key = np.arange(KEYS) % PIECE >= PIECE // 2
    query = np.arange(GROUP * SLOT) % SLOT >= PIECE // 2
    return np.where(key[:, None] != query[None, :], MASKED, 0.0).astype(np.float32)


def normed(values, gain_row):
    centered = values - jnp.mean(values, axis=-1, keepdims=True)
    spread = jnp.mean(centered * centered, axis=-1, keepdims=True)
    return centered * lax.rsqrt(spread + epsilon) * gain_row


def dot(left, right):
    return jnp.dot(left, right, preferred_element_type=jnp.float32)


def attend(windows):
    count = windows[0][0].shape[0]
    lane = lax.broadcasted_iota(jnp.int32, (count, LANES), 1)
    heads = [
        ((lane >= h * HEAD) & (lane < (h + 1) * HEAD)).astype(jnp.float32) for h in range(GROUP)
    ]
    heads = [head.astype(windows[0][0].dtype) for head in heads]
    scale = math.log2(math.e) / math.sqrt(HEAD)
    scores = []
    for query, key, _, bias in windows:
        stacked = jnp.concatenate([query * head for head in heads], axis=0).astype(jnp.bfloat16)
        score = lax.dot_general(
            key, stacked, (((1,), (1,)), ((), ())), preferred_element_type=jnp.float32
        )
        scores.append(score if bias is None else score + bias)
    probs = []
    for score in scores:
        weights = jnp.exp2((score - jnp.max(score, axis=0, keepdims=True)) * scale)
        total = jnp.sum(weights, axis=0, keepdims=True)
        probs.append((weights * (1.0 / total)).astype(jnp.bfloat16))
    mixed = [
        lax.dot_general(
            prob, window[2], (((0,), (0,)), ((), ())), preferred_element_type=jnp.float32
        )
        for prob, window in zip(probs, windows)
    ]
    contexts = []
    for mix in mixed:
        context = mix[:count]
        for h in range(1, GROUP):
            context = jnp.where(lane >= h * HEAD, mix[h * count : (h + 1) * count], context)
        contexts.append(context)
    return contexts


def by_rows(contexts, count):
    per = HEADS // GROUP
    return jnp.concatenate(
        [
            jnp.concatenate(contexts[start : start + per], axis=1)[:count]
            for start in range(0, len(contexts), per)
        ],
        axis=0,
    ).astype(jnp.bfloat16)


def stage(body):
    pl.when(lax.axis_index("lat") >= 0)(body)


def halves(ref):
    values = ref[...].astype(jnp.float32)
    return values[:QUAD], values[QUAD:]


def rounded(*parts):
    return jnp.concatenate(parts, axis=0).astype(jnp.bfloat16)


def _fetch(pairs, sems):
    copies = [
        pltpu.make_async_copy(source, target, sems.at[index])
        for index, (source, target) in enumerate(pairs)
    ]
    for copy in copies:
        copy.start()
    return copies


def window_kernel(
    x_hbm, to_win_hbm, gain_hbm, w_qkv_hbm, w_out_hbm, to_quad_hbm, gain_shift_hbm,
    w_next_hbm, bias_hbm, kept_ref, north_ref, south_ref, w_next_ref, bias_ref,
    x_ref, to_win_ref, gain_ref, w_qkv_ref, w_out_ref, to_quad_ref, gain_shift_ref, sems,
):
    odd = lax.rem(lax.axis_index("lon"), 2)
    copies = _fetch(
        (
            (x_hbm, x_ref), (to_win_hbm, to_win_ref), (gain_hbm, gain_ref),
            (w_qkv_hbm, w_qkv_ref), (w_out_hbm, w_out_ref),
            (to_quad_hbm.at[odd], to_quad_ref), (gain_shift_hbm, gain_shift_ref),
            (w_next_hbm, w_next_ref), (bias_hbm, bias_ref),
        ),
        sems,
    )
    for copy in copies[:3]:
        copy.wait()
    width = x_ref.shape[-1]
    x = x_ref[...].astype(jnp.float32).reshape(TOKENS, width).astype(jnp.bfloat16)
    x = dot(to_win_ref[...], x)
    tokens = normed(x, gain_ref[...]).astype(jnp.bfloat16)
    copies[3].wait()
    query, key, value = (
        dot(tokens, w_qkv_ref[:, part * width : (part + 1) * width]).astype(jnp.bfloat16)
        for part in range(3)
    )
    windows = []
    for w in range(TOKENS // WIN):
        rows = slice(w * WIN, (w + 1) * WIN)
        for g in range(HEADS // GROUP):
            cols = slice(g * LANES, (g + 1) * LANES)
            windows.append((query[rows, cols], key[rows, cols], value[rows, cols], None))
    context = by_rows(attend(windows), WIN)
    for copy in copies[4:7]:
        copy.wait()
    after = (x + dot(context, w_out_ref[...])).astype(jnp.bfloat16)
    after = dot(to_quad_ref[...], after)
    kept_ref[...] = after.astype(jnp.bfloat16)
    quads = normed(after, gain_shift_ref[...])
    for half, ref in enumerate((north_ref, south_ref)):
        ref[...] = rounded(
            *(quads[start : start + QUAD] for start in (half * QUAD, HALF + half * QUAD))
        )
    copies[7].wait()
    copies[8].wait()


def own_kernel(
    north_ref, south_ref, w_qkv_ref, query_ref, kv_ref, side_a_ref, side_b_ref
):
    (na, nb), (sa, sb) = halves(north_ref), halves(south_ref)
    side_a, side_b = rounded(na, sa), rounded(nb, sb)
    side_a_ref[...] = side_a
    side_b_ref[...] = side_b
    tokens = jnp.concatenate([side_a, side_b], axis=0)
    width = tokens.shape[-1]
    query_ref[:TOKENS] = dot(tokens, w_qkv_ref[:, :width])
    query_ref[TOKENS:] = jnp.zeros_like(query_ref[TOKENS:])
    kv_ref[...] = dot(tokens, w_qkv_ref[:, width:])


def side_context(side, query_ref, kv_ref, kv_near_ref, kv_corner_ref, bias_ref):
    width = query_ref.shape[-1]
    band = lax.axis_index("lat")
    place = lax.broadcasted_iota(jnp.int32, (KEYS, GROUP * SLOT), 0)
    across = ((place >= PIECE) & (place < 2 * PIECE)) | (place >= 3 * PIECE)
    windows = []
    for half in range(2):
        edge = band == (0 if half == 0 else lax.axis_size("lat") - 1)
        seam = jnp.where(across & edge, jnp.float32(MASKED), jnp.float32(0.0))
        own = side * HALF + half * QUAD
        for pair in range(2):
            bias = seam if pair == 0 else seam + bias_ref[...]
            at = pair * PIECE
            kv = rounded(
                *(
                    ref[start + at : start + at + PIECE]
                    for ref, start in (
                        (kv_ref, own), (kv_near_ref, half * QUAD),
                        (kv_near_ref, HALF + half * QUAD), (kv_corner_ref, half * QUAD),
                    )
                )
            )
            query = query_ref[own + at : own + at + SLOT]
            for g in range(HEADS // GROUP):
                cols = slice(g * LANES, (g + 1) * LANES)
                values = slice(width + g * LANES, width + (g + 1) * LANES)
                windows.append((query[:, cols], kv[:, cols], kv[:, values], bias))
    return by_rows(attend(windows), PIECE)


def block(context, kept, w_out, gain_mlp, w_up, w_down):
    branch = dot(context, w_out()).astype(jnp.bfloat16).astype(jnp.float32)
    shift = (kept.astype(jnp.float32) + branch).astype(jnp.bfloat16).astype(jnp.float32)
    tokens = normed(shift, gain_mlp()).astype(jnp.bfloat16)
    hidden = jax.nn.gelu(dot(tokens, w_up()), approximate=True).astype(jnp.bfloat16)
    return (shift + dot(hidden, w_down())).astype(jnp.bfloat16)


def near_kernel(
    north_ref, south_ref, side_a_ref, side_b_ref, corner_ref, kept_ref, query_ref, kv_ref,
    w_qkv_ref, bias_ref, w_out_hbm, gain_mlp_hbm, w_up_hbm, w_down_hbm,
    after_ref, kv_b_ref, w_out_ref, gain_mlp_ref, w_up_ref, w_down_ref,
    kv_a_ref, kv_corner_ref, context_ref, sems,
):
    pairs = (
        (w_out_hbm, w_out_ref), (gain_mlp_hbm, gain_mlp_ref), (w_up_hbm, w_up_ref),
        (w_down_hbm, w_down_ref),
    )
    copies = _fetch(pairs, sems)

    def arrived(index):
        def array():
            copies[index].wait()
            return pairs[index][1][...]

        return array

    width = query_ref.shape[-1]

    @stage
    def _():
        (north_a, north_b), (south_a, south_b) = halves(north_ref), halves(south_ref)
        tokens = jnp.concatenate(
            [
                rounded(north_a, south_a), side_a_ref[...], corner_ref[...],
                rounded(north_b, south_b), side_b_ref[...],
            ],
            axis=0,
        )
        halo = dot(tokens, w_qkv_ref[:, width:])
        kv_a_ref[...] = halo[:TOKENS]
        kv_corner_ref[...] = halo[TOKENS : TOKENS + HALF]
        kv_b_ref[...] = halo[TOKENS + HALF :]

    @stage
    def _():
        context_ref[...] = side_context(0, query_ref, kv_ref, kv_a_ref, kv_corner_ref, bias_ref)

    after_ref[...] = block(context_ref[...], kept_ref[:HALF], *map(arrived, range(4)))


def last_kernel(
    corner_ref, kept_ref, after_ref, query_ref, kv_ref, kv_b_ref, w_qkv_ref, bias_ref,
    w_out_ref, gain_mlp_ref, w_up_ref, w_down_ref, to_merge_hbm, gain_merge_hbm, w_merge_hbm,
    out_ref, kv_corner_ref, context_ref, to_merge_ref, gain_merge_ref, w_merge_ref, sems,
):
    odd = lax.rem(lax.axis_index("lon"), 2)
    copies = _fetch(
        (
            (to_merge_hbm.at[odd], to_merge_ref), (gain_merge_hbm, gain_merge_ref),
            (w_merge_hbm, w_merge_ref),
        ),
        sems,
    )
    width = kept_ref.shape[-1]

    @stage
    def _():
        kv_corner_ref[...] = dot(corner_ref[...], w_qkv_ref[:, width:])

    @stage
    def _():
        context_ref[...] = side_context(1, query_ref, kv_ref, kv_b_ref, kv_corner_ref, bias_ref)

    weights = (w_out_ref, gain_mlp_ref, w_up_ref, w_down_ref)
    after = block(
        context_ref[...], kept_ref[HALF:], *(lambda ref=ref: ref[...] for ref in weights)
    )
    copies[0].wait()
    merge = dot(to_merge_ref[...], jnp.concatenate([after_ref[...], after], axis=0))
    stacked = jnp.concatenate([merge[i * QUAD : (i + 1) * QUAD] for i in range(4)], axis=1)
    copies[1].wait()
    tokens = normed(stacked, gain_merge_ref[...]).astype(jnp.bfloat16)
    copies[2].wait()
    merged = dot(tokens, w_merge_ref[...])
    out_ref[...] = merged.reshape(out_ref.shape).astype(jnp.bfloat16)


def _in_hbm(array):
    return pltpu.with_memory_space_constraint(array, pltpu.HBM)


def _call(kernel, near, far, outs, scratch=(), copies=0, flops=0):
    near_spec, far_spec = pl.BlockSpec(memory_space=pltpu.VMEM), pl.BlockSpec(memory_space=pltpu.HBM)
    return pl.pallas_call(
        kernel,
        out_shape=outs,
        in_specs=[near_spec] * len(near) + [far_spec] * len(far),
        out_specs=jax.tree.map(lambda _: near_spec, outs),
        scratch_shapes=list(scratch) + ([pltpu.SemaphoreType.DMA((copies,))] if copies else []),
        compiler_params=pltpu.CompilerParams(vmem_limit_bytes=VMEM_BYTES),
        cost_estimate=pl.CostEstimate(flops=flops, bytes_accessed=0, transcendentals=0),
    )(*near, *map(_in_hbm, far))


def _vmem(array):
    return pltpu.VMEM(array.shape, array.dtype)


def _rows(value, step):
    count = lax.axis_size("lat")
    return lax.ppermute(value, "lat", [((i + step) % count, i) for i in range(count)])


def _swap(value, first):
    count = lax.axis_size("lon")
    pairs = [(j % count, (j + 1) % count) for j in range(first, count + first, 2)]
    return lax.ppermute(value, "lon", pairs + [(b, a) for a, b in pairs])


def on_device(
    latent_field, gain_win, w_qkv_win, w_out_win, gain_shift, w_qkv_shift, w_out_shift,
    gain_mlp, w_up, w_down, gain_merge, w_merge,
):
    width = latent_field.shape[-1]
    natural, windows, merges = _natural_tokens(), _window_tokens(), _merge_tokens()
    quads = [_quadrant_tokens(odd) for odd in (False, True)]
    to_win = jnp.asarray(_permutation(windows, natural), jnp.bfloat16)
    to_quad = jnp.asarray(np.stack([_permutation(q, windows) for q in quads]), jnp.bfloat16)
    to_merge = jnp.asarray(np.stack([_permutation(merges, q) for q in quads]), jnp.bfloat16)
    bias = jnp.asarray(_bias())
    gain_win, gain_shift, gain_mlp, gain_merge = (
        gain.reshape(1, -1) for gain in (gain_win, gain_shift, gain_mlp, gain_merge)
    )

    def bf16(rows, cols=width):
        return pltpu.VMEM((rows, cols), jnp.bfloat16)

    def f32(rows, cols):
        return pltpu.VMEM((rows, cols), jnp.float32)

    x = latent_field.reshape(WLAT * WLON, LEV, width)
    first = (x, to_win, gain_win, w_qkv_win, w_out_win, to_quad, gain_shift, w_qkv_shift, bias)
    held = [_vmem(array) for array in first[:-2]]
    held[5] = bf16(TOKENS, TOKENS)
    kept, north, south, w_qkv, bias = _call(
        window_kernel, (), first,
        (bf16(TOKENS), bf16(HALF), bf16(HALF), _vmem(w_qkv_shift), _vmem(bias)), held, len(first),
    )
    from_north = _rows(south, -1)
    from_south = _rows(north, 1)
    query, kv, side_a, side_b = _call(
        own_kernel, (north, south, w_qkv), (),
        (f32(TOKENS + 8, width), f32(TOKENS, 2 * width), bf16(HALF), bf16(HALF)),
    )
    from_a = _swap(side_a, 0)
    from_b = _swap(side_b, 1)
    corner_a = _swap(jnp.concatenate([from_north[:QUAD], from_south[:QUAD]], axis=0), 0)
    corner_b = _swap(jnp.concatenate([from_north[QUAD:], from_south[QUAD:]], axis=0), 1)
    far = (w_out_shift, gain_mlp, w_up, w_down)
    after, kv_b, *weights = _call(
        near_kernel,
        (from_north, from_south, from_a, from_b, corner_a, kept, query, kv, w_qkv, bias), far,
        (bf16(HALF), f32(TOKENS, 2 * width), *map(_vmem, far)),
        (f32(TOKENS, 2 * width), f32(HALF, 2 * width), bf16(HALF)), len(far), flops=10**11,
    )
    merged = _call(
        last_kernel, (corner_b, kept, after, query, kv, kv_b, w_qkv, bias, *weights),
        (to_merge, gain_merge, w_merge),
        jax.ShapeDtypeStruct((QUAD // LEV, LEV, 2 * width), jnp.bfloat16),
        (
            f32(HALF, 2 * width), bf16(HALF), bf16(TOKENS, TOKENS), _vmem(gain_merge), _vmem(w_merge),
        ),
        3,
    )
    return merged.reshape(WLAT // 2, WLON // 2, LEV, 2 * width)


def solution(mesh):
    in_specs = (P("lat", "lon", None, None),) + (P(),) * 11
    return jax.shard_map(
        on_device,
        mesh=mesh,
        in_specs=in_specs,
        out_specs=P("lat", "lon", None, None),
        check_vma=False,
    )
```

```python
import math

import jax
import jax.numpy as jnp
import numpy as np
from jax import lax
from jax.experimental import pallas as pl
from jax.experimental.pallas import tpu as pltpu
from jax.sharding import PartitionSpec as P

HEADS = 16
HEAD = 32
WLAT = 6
WLON = 12
WLEV = 2
LEV = 4
HALF_LAT = WLAT // 2
HALF_LON = WLON // 2
WIN = WLAT * WLON * WLEV
TOKENS = WLAT * WLON * LEV
QUAD = TOKENS // 4
GROUP = 8
LANES = GROUP * HEAD
PIECE = QUAD // 2
SLOT = 40
KEYS = 4 * PIECE
HALF = 2 * QUAD
VMEM_BYTES = 28 * 1024 * 1024
MASKED = -1e30

epsilon = 1e-05


def _natural_tokens():
    return [(r, c, l) for r in range(WLAT) for c in range(WLON) for l in range(LEV)]


def _window_tokens():
    return [(r, c, l) for l in range(LEV) for r in range(WLAT) for c in range(WLON)]


def _quadrant_tokens(odd):
    sides = (0, 1) if odd else (1, 0)
    tokens = []
    for side in sides:
        for half in range(2):
            for pair in ((1, 2), (3, 0)):
                tokens += [
                    (half * HALF_LAT + r, side * HALF_LON + c, l)
                    for l in pair
                    for r in range(HALF_LAT)
                    for c in range(HALF_LON)
                ]
    return tokens


def _merge_tokens():
    return [
        (2 * i + piece % 2, 2 * j + piece // 2, l)
        for piece in range(4)
        for i in range(WLAT // 2)
        for j in range(WLON // 2)
        for l in range(LEV)
    ]


def _permutation(target, source):
    place = {token: index for index, token in enumerate(source)}
    matrix = np.zeros((len(target), len(source)), np.float32)
    for index, token in enumerate(target):
        matrix[index, place[token]] = 1.0
    return matrix


def _bias():
    key = np.arange(KEYS) % PIECE >= PIECE // 2
    query = np.arange(GROUP * SLOT) % SLOT >= PIECE // 2
    return np.where(key[:, None] != query[None, :], MASKED, 0.0).astype(np.float32)


def normed(values, gain_row):
    centered = values - jnp.mean(values, axis=-1, keepdims=True)
    spread = jnp.mean(centered * centered, axis=-1, keepdims=True)
    return centered * lax.rsqrt(spread + epsilon) * gain_row


def dot(left, right):
    return jnp.dot(left, right, preferred_element_type=jnp.float32)


def attend(windows):
    count = windows[0][0].shape[0]
    lane = lax.broadcasted_iota(jnp.int32, (count, LANES), 1)
    heads = [
        ((lane >= h * HEAD) & (lane < (h + 1) * HEAD)).astype(jnp.float32) for h in range(GROUP)
    ]
    heads = [head.astype(windows[0][0].dtype) for head in heads]
    scale = math.log2(math.e) / math.sqrt(HEAD)
    scores = []
    for query, key, _, bias in windows:
        stacked = jnp.concatenate([query * head for head in heads], axis=0).astype(jnp.bfloat16)
        score = lax.dot_general(
            key, stacked, (((1,), (1,)), ((), ())), preferred_element_type=jnp.float32
        )
        scores.append(score if bias is None else score + bias)
    probs = []
    for score in scores:
        weights = jnp.exp2((score - jnp.max(score, axis=0, keepdims=True)) * scale)
        total = jnp.sum(weights, axis=0, keepdims=True)
        probs.append((weights * (1.0 / total)).astype(jnp.bfloat16))
    mixed = [
        lax.dot_general(
            prob, window[2], (((0,), (0,)), ((), ())), preferred_element_type=jnp.float32
        )
        for prob, window in zip(probs, windows)
    ]
    contexts = []
    for mix in mixed:
        context = mix[:count]
        for h in range(1, GROUP):
            context = jnp.where(lane >= h * HEAD, mix[h * count : (h + 1) * count], context)
        contexts.append(context)
    return contexts


def by_rows(contexts, count):
    per = HEADS // GROUP
    return jnp.concatenate(
        [
            jnp.concatenate(contexts[start : start + per], axis=1)[:count]
            for start in range(0, len(contexts), per)
        ],
        axis=0,
    ).astype(jnp.bfloat16)


def stage(body):
    pl.when(lax.axis_index("lat") >= 0)(body)


def halves(ref):
    values = ref[...].astype(jnp.float32)
    return values[:QUAD], values[QUAD:]


def rounded(*parts):
    return jnp.concatenate(parts, axis=0).astype(jnp.bfloat16)


def _fetch(pairs, sems):
    copies = [
        pltpu.make_async_copy(source, target, sems.at[index])
        for index, (source, target) in enumerate(pairs)
    ]
    for copy in copies:
        copy.start()
    return copies


def window_kernel(
    x_hbm, to_win_hbm, gain_hbm, w_qkv_hbm, w_out_hbm, to_quad_hbm, gain_shift_hbm,
    w_next_hbm, bias_hbm, kept_ref, north_ref, south_ref, w_next_ref, bias_ref,
    x_ref, to_win_ref, gain_ref, w_qkv_ref, w_out_ref, to_quad_ref, gain_shift_ref, sems,
):
    odd = lax.rem(lax.axis_index("lon"), 2)
    copies = _fetch(
        (
            (x_hbm, x_ref), (to_win_hbm, to_win_ref), (gain_hbm, gain_ref),
            (w_qkv_hbm, w_qkv_ref), (w_out_hbm, w_out_ref),
            (to_quad_hbm.at[odd], to_quad_ref), (gain_shift_hbm, gain_shift_ref),
            (w_next_hbm, w_next_ref), (bias_hbm, bias_ref),
        ),
        sems,
    )
    copies[0].wait()
    width = x_ref.shape[-1]
    x = x_ref[...].astype(jnp.float32).reshape(TOKENS, width).astype(jnp.bfloat16)
    copies[1].wait()
    x = dot(to_win_ref[...], x)
    copies[2].wait()
    tokens = normed(x, gain_ref[...]).astype(jnp.bfloat16)
    copies[3].wait()
    query, key, value = (
        dot(tokens, w_qkv_ref[:, part * width : (part + 1) * width]).astype(jnp.bfloat16)
        for part in range(3)
    )
    windows = []
    for w in range(TOKENS // WIN):
        rows = slice(w * WIN, (w + 1) * WIN)
        for g in range(HEADS // GROUP):
            cols = slice(g * LANES, (g + 1) * LANES)
            windows.append((query[rows, cols], key[rows, cols], value[rows, cols], None))
    context = by_rows(attend(windows), WIN)
    for copy in copies[4:7]:
        copy.wait()
    after = (x + dot(context, w_out_ref[...])).astype(jnp.bfloat16)
    after = dot(to_quad_ref[...], after)
    kept_ref[...] = after.astype(jnp.bfloat16)
    quads = normed(after, gain_shift_ref[...])
    for half, ref in enumerate((north_ref, south_ref)):
        ref[...] = rounded(
            *(quads[start : start + QUAD] for start in (half * QUAD, HALF + half * QUAD))
        )
    copies[7].wait()
    copies[8].wait()


def own_kernel(
    north_ref, south_ref, w_qkv_ref, query_ref, kv_ref, side_a_ref, side_b_ref
):
    (na, nb), (sa, sb) = halves(north_ref), halves(south_ref)
    side_a, side_b = rounded(na, sa), rounded(nb, sb)
    side_a_ref[...] = side_a
    side_b_ref[...] = side_b
    tokens = jnp.concatenate([side_a, side_b], axis=0)
    width = tokens.shape[-1]
    query_ref[:TOKENS] = dot(tokens, w_qkv_ref[:, :width])
    query_ref[TOKENS:] = jnp.zeros_like(query_ref[TOKENS:])
    kv_ref[...] = dot(tokens, w_qkv_ref[:, width:])


def side_context(side, query_ref, kv_ref, kv_near_ref, kv_corner_ref, bias_ref):
    width = query_ref.shape[-1]
    band = lax.axis_index("lat")
    place = lax.broadcasted_iota(jnp.int32, (KEYS, GROUP * SLOT), 0)
    across = ((place >= PIECE) & (place < 2 * PIECE)) | (place >= 3 * PIECE)
    windows = []
    for half in range(2):
        edge = band == (0 if half == 0 else lax.axis_size("lat") - 1)
        seam = jnp.where(across & edge, jnp.float32(MASKED), jnp.float32(0.0))
        own = side * HALF + half * QUAD
        for pair in range(2):
            bias = seam if pair == 0 else seam + bias_ref[...]
            at = pair * PIECE
            kv = rounded(
                *(
                    ref[start + at : start + at + PIECE]
                    for ref, start in (
                        (kv_ref, own), (kv_near_ref, half * QUAD),
                        (kv_near_ref, HALF + half * QUAD), (kv_corner_ref, half * QUAD),
                    )
                )
            )
            query = query_ref[own + at : own + at + SLOT]
            for g in range(HEADS // GROUP):
                cols = slice(g * LANES, (g + 1) * LANES)
                values = slice(width + g * LANES, width + (g + 1) * LANES)
                windows.append((query[:, cols], kv[:, cols], kv[:, values], bias))
    return by_rows(attend(windows), PIECE)


def block(context, kept, w_out, gain_mlp, w_up, w_down):
    branch = dot(context, w_out()).astype(jnp.bfloat16).astype(jnp.float32)
    shift = (kept.astype(jnp.float32) + branch).astype(jnp.bfloat16).astype(jnp.float32)
    tokens = normed(shift, gain_mlp()).astype(jnp.bfloat16)
    hidden = jax.nn.gelu(dot(tokens, w_up()), approximate=True).astype(jnp.bfloat16)
    return (shift + dot(hidden, w_down())).astype(jnp.bfloat16)


def near_kernel(
    north_ref, south_ref, side_a_ref, side_b_ref, corner_ref, kept_ref, query_ref, kv_ref,
    w_qkv_ref, bias_ref, w_out_hbm, gain_mlp_hbm, w_up_hbm, w_down_hbm,
    after_ref, kv_b_ref, w_out_ref, gain_mlp_ref, w_up_ref, w_down_ref,
    kv_a_ref, kv_corner_ref, context_ref, sems,
):
    pairs = (
        (w_out_hbm, w_out_ref), (gain_mlp_hbm, gain_mlp_ref), (w_up_hbm, w_up_ref),
        (w_down_hbm, w_down_ref),
    )
    copies = _fetch(pairs, sems)

    def arrived(index):
        def array():
            copies[index].wait()
            return pairs[index][1][...]

        return array

    width = query_ref.shape[-1]

    @stage
    def _():
        (north_a, north_b), (south_a, south_b) = halves(north_ref), halves(south_ref)
        tokens = jnp.concatenate(
            [
                rounded(north_a, south_a), side_a_ref[...], corner_ref[...],
                rounded(north_b, south_b), side_b_ref[...],
            ],
            axis=0,
        )
        halo = dot(tokens, w_qkv_ref[:, width:])
        kv_a_ref[...] = halo[:TOKENS]
        kv_corner_ref[...] = halo[TOKENS : TOKENS + HALF]
        kv_b_ref[...] = halo[TOKENS + HALF :]

    @stage
    def _():
        context_ref[...] = side_context(0, query_ref, kv_ref, kv_a_ref, kv_corner_ref, bias_ref)

    after_ref[...] = block(context_ref[...], kept_ref[:HALF], *map(arrived, range(4)))


def last_kernel(
    corner_ref, kept_ref, after_ref, query_ref, kv_ref, kv_b_ref, w_qkv_ref, bias_ref,
    w_out_ref, gain_mlp_ref, w_up_ref, w_down_ref, to_merge_hbm, gain_merge_hbm, w_merge_hbm,
    out_ref, kv_corner_ref, context_ref, to_merge_ref, gain_merge_ref, w_merge_ref, sems,
):
    odd = lax.rem(lax.axis_index("lon"), 2)
    copies = _fetch(
        (
            (to_merge_hbm.at[odd], to_merge_ref), (gain_merge_hbm, gain_merge_ref),
            (w_merge_hbm, w_merge_ref),
        ),
        sems,
    )
    width = kept_ref.shape[-1]

    @stage
    def _():
        kv_corner_ref[...] = dot(corner_ref[...], w_qkv_ref[:, width:])

    @stage
    def _():
        context_ref[...] = side_context(1, query_ref, kv_ref, kv_b_ref, kv_corner_ref, bias_ref)

    weights = (w_out_ref, gain_mlp_ref, w_up_ref, w_down_ref)
    after = block(
        context_ref[...], kept_ref[HALF:], *(lambda ref=ref: ref[...] for ref in weights)
    )
    copies[0].wait()
    merge = dot(to_merge_ref[...], jnp.concatenate([after_ref[...], after], axis=0))
    stacked = jnp.concatenate([merge[i * QUAD : (i + 1) * QUAD] for i in range(4)], axis=1)
    copies[1].wait()
    tokens = normed(stacked, gain_merge_ref[...]).astype(jnp.bfloat16)
    copies[2].wait()
    merged = dot(tokens, w_merge_ref[...])
    out_ref[...] = merged.reshape(out_ref.shape).astype(jnp.bfloat16)


def _in_hbm(array):
    return pltpu.with_memory_space_constraint(array, pltpu.HBM)


def _call(kernel, near, far, outs, scratch=(), copies=0, flops=0):
    near_spec, far_spec = pl.BlockSpec(memory_space=pltpu.VMEM), pl.BlockSpec(memory_space=pltpu.HBM)
    return pl.pallas_call(
        kernel,
        out_shape=outs,
        in_specs=[near_spec] * len(near) + [far_spec] * len(far),
        out_specs=jax.tree.map(lambda _: near_spec, outs),
        scratch_shapes=list(scratch) + ([pltpu.SemaphoreType.DMA((copies,))] if copies else []),
        compiler_params=pltpu.CompilerParams(vmem_limit_bytes=VMEM_BYTES),
        cost_estimate=pl.CostEstimate(flops=flops, bytes_accessed=0, transcendentals=0),
    )(*near, *map(_in_hbm, far))


def _vmem(array):
    return pltpu.VMEM(array.shape, array.dtype)


def _rows(value, step):
    count = lax.axis_size("lat")
    return lax.ppermute(value, "lat", [((i + step) % count, i) for i in range(count)])


def _swap(value, first):
    count = lax.axis_size("lon")
    pairs = [(j % count, (j + 1) % count) for j in range(first, count + first, 2)]
    return lax.ppermute(value, "lon", pairs + [(b, a) for a, b in pairs])


def on_device(
    latent_field, gain_win, w_qkv_win, w_out_win, gain_shift, w_qkv_shift, w_out_shift,
    gain_mlp, w_up, w_down, gain_merge, w_merge,
):
    width = latent_field.shape[-1]
    natural, windows, merges = _natural_tokens(), _window_tokens(), _merge_tokens()
    quads = [_quadrant_tokens(odd) for odd in (False, True)]
    to_win = jnp.asarray(_permutation(windows, natural), jnp.bfloat16)
    to_quad = jnp.asarray(np.stack([_permutation(q, windows) for q in quads]), jnp.bfloat16)
    to_merge = jnp.asarray(np.stack([_permutation(merges, q) for q in quads]), jnp.bfloat16)
    bias = jnp.asarray(_bias())
    gain_win, gain_shift, gain_mlp, gain_merge = (
        gain.reshape(1, -1) for gain in (gain_win, gain_shift, gain_mlp, gain_merge)
    )

    def bf16(rows, cols=width):
        return pltpu.VMEM((rows, cols), jnp.bfloat16)

    def f32(rows, cols):
        return pltpu.VMEM((rows, cols), jnp.float32)

    x = latent_field.reshape(WLAT * WLON, LEV, width)
    first = (x, to_win, gain_win, w_qkv_win, w_out_win, to_quad, gain_shift, w_qkv_shift, bias)
    held = [_vmem(array) for array in first[:-2]]
    held[5] = bf16(TOKENS, TOKENS)
    kept, north, south, w_qkv, bias = _call(
        window_kernel, (), first,
        (bf16(TOKENS), bf16(HALF), bf16(HALF), _vmem(w_qkv_shift), _vmem(bias)), held, len(first),
    )
    from_north = _rows(south, -1)
    from_south = _rows(north, 1)
    query, kv, side_a, side_b = _call(
        own_kernel, (north, south, w_qkv), (),
        (f32(TOKENS + 8, width), f32(TOKENS, 2 * width), bf16(HALF), bf16(HALF)),
    )
    from_a = _swap(side_a, 0)
    from_b = _swap(side_b, 1)
    corner_a = _swap(jnp.concatenate([from_north[:QUAD], from_south[:QUAD]], axis=0), 0)
    corner_b = _swap(jnp.concatenate([from_north[QUAD:], from_south[QUAD:]], axis=0), 1)
    far = (w_out_shift, gain_mlp, w_up, w_down)
    after, kv_b, *weights = _call(
        near_kernel,
        (from_north, from_south, from_a, from_b, corner_a, kept, query, kv, w_qkv, bias), far,
        (bf16(HALF), f32(TOKENS, 2 * width), *map(_vmem, far)),
        (f32(TOKENS, 2 * width), f32(HALF, 2 * width), bf16(HALF)), len(far), flops=10**11,
    )
    merged = _call(
        last_kernel, (corner_b, kept, after, query, kv, kv_b, w_qkv, bias, *weights),
        (to_merge, gain_merge, w_merge),
        jax.ShapeDtypeStruct((QUAD // LEV, LEV, 2 * width), jnp.bfloat16),
        (
            f32(HALF, 2 * width), bf16(HALF), bf16(TOKENS, TOKENS), _vmem(gain_merge), _vmem(w_merge),
        ),
        3,
    )
    return merged.reshape(WLAT // 2, WLON // 2, LEV, 2 * width)


def solution(mesh):
    in_specs = (P("lat", "lon", None, None),) + (P(),) * 11
    return jax.shard_map(
        on_device,
        mesh=mesh,
        in_specs=in_specs,
        out_specs=P("lat", "lon", None, None),
        check_vma=False,
    )
```
